256 devices in a mesh: tm: 32 (over y, z_lo, core), rows: 8 (over x, z_hi).
Axes of the slice: x: 4, y: 4, z: 8 (z_hi: 2, z_lo: 4; z = z_hi * 4 + z_lo), core: 2. Of those that a mesh axis runs over, the one named last changes fastest.
Arguments:
- noisy_states: float32 [128, 2, 64, 256], P('tm', None, 'rows'), may hold values from -6 to 6
- noise_first: float32 [128, 2, 64, 256], P('tm', None, 'rows'), may hold values from -6 to 6
- noise_second: float32 [128, 2, 64, 256], P('tm', None, 'rows'), may hold values from -6 to 6
- conv_in: bfloat16 [9, 96, 18], replicated, may hold values from -0.5 to 0.5
- conv_out: bfloat16 [9, 2, 96], replicated, may hold values from -0.21875 to 0.21875
- level_embed: float32 [96], replicated, may hold values from -4 to 4
- obs_count: int32 [32, 8], P('tm', 'rows'), may hold values from 1 to 256, as said below
- obs_step: int32 [32, 8, 256], P('tm', 'rows'), may hold values from 0 to 3
- obs_row: int32 [32, 8, 256], P('tm', 'rows'), may hold values from 0 to 7
- obs_col: int32 [32, 8, 256], P('tm', 'rows'), may hold values from 0 to 255
- obs_value: float32 [32, 8, 256], P('tm', 'rows'), may hold values from -4 to 4
Outputs:
- final_states: float32 [128, 2, 64, 256], P('tm', None, 'rows')
The draws below stay inside these ranges and needn't reach their ends.
Inputs may be any that keep to these rules, and one draw needn't show every extreme that they name: `obs_count`: some block has exactly 256 live observations in every draw; the counts are skewed over blocks.
All inputs are finite; a program needn't handle non-finite values.
Results may differ from the reference program's by a relative error of at most 0.0014.
Values may be sent and summed in bfloat16 or wider, within the bound.
A program may use at most 64 MiB of HBM per device.

```python
import jax
import jax.numpy as jnp
from jax import lax

T_DEV = 4
ROWS_DEV = 8
OBS_CAP = 256
COLS = 256
LAYERS = 2
K = 4
HID = 96
C_IN = 18
STEPS = 128
NY = 64
N_TM = 32
N_ROWS = 8


def draw_obs_count(key, part):
    first_key, second_key, third_key = jax.random.split(jax.random.fold_in(key, 17), 3)
    base_count = jax.random.randint(first_key, (N_TM * N_ROWS,), 1, OBS_CAP // 8 + 1)
    dense_pick = jax.random.randint(second_key, (N_TM * N_ROWS,), 0, 4)
    counts = jnp.minimum(base_count * jnp.where(dense_pick == 3, 8, 1), OBS_CAP)
    full_block = jax.random.randint(third_key, (), 0, N_TM * N_ROWS)
    counts = counts.at[full_block].set(OBS_CAP)
    return counts.reshape(N_TM, N_ROWS).astype(jnp.int32)


def plant(result, rng, smallest, largest):
    longest = result.shape.index(max(result.shape))
    spots = []
    for shift in (0, 1):
        where = [jax.random.randint(jax.random.fold_in(rng, axis), (), 0, length) for axis, length in enumerate(result.shape)]
        where[longest] = (where[longest] + shift) % result.shape[longest]
        spots.append(tuple(where))
    return result.at[spots[0]].set(smallest).at[spots[1]].set(largest)


def levels(stream_key, extent, cuts, low, largest):
    level, own = 1.0, jax.random.fold_in(stream_key, 6)
    for axis_at, shards_of in cuts:
        draws = jnp.exp(jax.random.uniform(jax.random.fold_in(own, axis_at), (shards_of,), jnp.float32, low / len(cuts), largest / len(cuts)))
        level = level * jnp.repeat(draws, extent[axis_at] // shards_of).reshape([-1 if axis == axis_at else 1 for axis in range(len(extent))])
    return level


def gaussian(key, shape, scale, limit, cuts=(), kind=jnp.bfloat16):
    loudness = levels(key, shape, cuts, -0.22, 0.18) if cuts else 1.0
    array = jax.random.normal(key, shape, jnp.float32) * scale * loudness
    return jnp.minimum(jnp.maximum(array, -limit), limit).astype(kind)


def setup_inputs(seed: int = 0) -> dict:
    arg_keys = jax.random.split(jax.random.key(seed), 12)
    return {
        "noisy_states": gaussian(arg_keys[0], (STEPS, LAYERS, NY, COLS), 1.0, 6.0, ((0, 32), (2, 8)), jnp.float32),
        "noise_first": gaussian(arg_keys[1], (STEPS, LAYERS, NY, COLS), 1.0, 6.0, ((0, 32), (2, 8)), jnp.float32),
        "noise_second": gaussian(arg_keys[2], (STEPS, LAYERS, NY, COLS), 1.0, 6.0, ((0, 32), (2, 8)), jnp.float32),
        "conv_in": gaussian(arg_keys[3], (9, HID, C_IN), (9 * C_IN) ** -0.5, 0.5),
        "conv_out": gaussian(arg_keys[4], (9, LAYERS, HID), (9 * HID) ** -0.5, 0.21875),
        "level_embed": gaussian(arg_keys[5], (HID,), 1.0, 4.0, (), jnp.float32),
        "obs_count": draw_obs_count(jax.random.fold_in(arg_keys[11], 71), 0),
        "obs_step": plant(jax.random.randint(arg_keys[7], (N_TM, N_ROWS, OBS_CAP), 0, T_DEV), jax.random.fold_in(arg_keys[7], 1), 0, T_DEV - 1).astype(jnp.int32),
        "obs_row": plant(jax.random.randint(arg_keys[8], (N_TM, N_ROWS, OBS_CAP), 0, ROWS_DEV), jax.random.fold_in(arg_keys[8], 1), 0, ROWS_DEV - 1).astype(jnp.int32),
        "obs_col": plant(jax.random.randint(arg_keys[9], (N_TM, N_ROWS, OBS_CAP), 0, COLS), jax.random.fold_in(arg_keys[9], 1), 0, COLS - 1).astype(jnp.int32),
        "obs_value": gaussian(arg_keys[10], (N_TM, N_ROWS, OBS_CAP), 1.0, 4.0, ((0, 32), (1, 8)), jnp.float32),
    }


LEVELS = (1.0, 0.5, 0.2)
OBS_NOISE = 0.1
COVARIANCE_GAIN = 0.5

def conv_periodic(window, weights):
    summed = jnp.zeros((weights.shape[1], window.shape[1], window.shape[2]), jnp.float32)
    for row_off in range(3):
        for col_off in range(3):
            shifted = jnp.roll(window, (1 - row_off, 1 - col_off), axis=(1, 2))
            summed = summed + jnp.einsum('oc,crw->orw', weights[3 * row_off + col_off].astype(jnp.float32), shifted.astype(jnp.float32))
    return summed

def reverse_step(current, noise_draw, level_now, level_next, conv_in, conv_out, level_embed, obs_count, obs_step, obs_row, obs_col, obs_value):
    scaled = (current / jnp.sqrt(1.0 + level_now ** 2)).astype(jnp.bfloat16)
    padded = jnp.pad(scaled, ((K, K), (0, 0), (0, 0), (0, 0)))

    def per_state(position):
        window = lax.dynamic_slice_in_dim(padded, position, 2 * K + 1, 0).reshape(C_IN, NY, COLS)
        hidden = jax.nn.silu(conv_periodic(window, conv_in) + level_now * level_embed[:, None, None]).astype(jnp.bfloat16)
        return conv_periodic(hidden, conv_out)
    net = lax.map(per_state, jnp.arange(STEPS, dtype=jnp.int32))
    denoised = current / (1.0 + level_now ** 2) + level_now / jnp.sqrt(1.0 + level_now ** 2) * net
    global_step = obs_step + (jnp.arange(N_TM, dtype=jnp.int32) * T_DEV)[:, None, None]
    global_row = obs_row + (jnp.arange(N_ROWS, dtype=jnp.int32) * ROWS_DEV)[None, :, None]
    active_slot = jnp.arange(OBS_CAP, dtype=jnp.int32)[None, None, :] < obs_count[:, :, None]
    picked = denoised[global_step, 0, global_row, obs_col]
    misfit = jnp.where(active_slot, (obs_value - picked) / (OBS_NOISE + COVARIANCE_GAIN * level_now ** 2), jnp.float32(0.0))
    guide = jnp.zeros(current.shape, jnp.float32).at[global_step, 0, global_row, obs_col].add(misfit)
    score = (denoised - current) / level_now ** 2 + guide
    spread = level_now ** 2 - level_next ** 2
    return current + spread * score + spread ** 0.5 * noise_draw

def reference(noisy_states, noise_first, noise_second, conv_in, conv_out, level_embed, obs_count, obs_step, obs_row, obs_col, obs_value):
    current = noisy_states
    for index_level, noise_draw in enumerate((noise_first, noise_second)):
        current = reverse_step(current, noise_draw, LEVELS[index_level], LEVELS[index_level + 1], conv_in, conv_out, level_embed, obs_count, obs_step, obs_row, obs_col, obs_value)
    return current
```

```python
import functools

import jax
import jax.numpy as jnp
from jax import lax
from jax.experimental import pallas as pl
from jax.experimental.pallas import tpu as pltpu
from jax.sharding import PartitionSpec as P

MESH = pl.DeviceIdType.MESH
LEVELS = (1.0, 0.5, 0.2)
OBS_NOISE = 0.1
COVARIANCE_GAIN = 0.5
T = 4
LAYERS = 2
TL = 8
ROWS = 8
COLS = 256
HID = 96
C_IN = 18
SLOTS = 256
PAIRS = 6
BANDS = 10
K_IN = 224
SENDS = ((-1, -1), (0, -1), (1, -1), (-1, 1), (0, 1), (1, 1), (-1, 0), (1, 0))


def three_parts(values):
    high = values.astype(jnp.bfloat16).astype(jnp.float32)
    rest = values - high
    mid = rest.astype(jnp.bfloat16).astype(jnp.float32)
    return high, mid, rest - mid


def build_conv_in(w1_raw, embed_raw, w1):
    lane = lax.broadcasted_iota(jnp.int32, (HID, 256), 1)
    base = jnp.zeros((HID, 256), jnp.float32)
    for off in range(9):
        slab = jnp.concatenate(
            [w1_raw[off].astype(jnp.float32) * 0.5, jnp.zeros((HID, 256 - C_IN), jnp.float32)], axis=1
        )
        base = base + (pltpu.roll(slab, 24 * off, 1) if off else slab)
    diagonal = lax.broadcasted_iota(jnp.int32, (HID, HID), 0) == lax.broadcasted_iota(
        jnp.int32, (HID, HID), 1
    )
    embed = jnp.sum(
        jnp.where(diagonal, jnp.broadcast_to(embed_raw[...], (HID, HID)), 0.0), axis=1, keepdims=True
    )
    parts = three_parts(embed * 0.5)
    for t in range(T):
        shifted = pltpu.roll(base, 2 * t, 1) if t else base
        for piece in range(3):
            shifted = jnp.where(lane == 216 + piece, parts[piece], shifted)
        w1[t * HID : (t + 1) * HID, :] = shifted[:, :K_IN].astype(jnp.bfloat16)


def build_conv_out(w2_raw, w2):
    sub = lax.broadcasted_iota(jnp.int32, (TL, HID), 0)
    pieces = []
    for b in range(3):
        for a in range(3):
            taps = w2_raw[3 * a + b].astype(jnp.float32)
            pieces.append(
                jnp.where(
                    sub % 2 == 0,
                    jnp.broadcast_to(taps[0:1], (TL, HID)),
                    jnp.broadcast_to(taps[1:2], (TL, HID)),
                )
            )
    tall = jnp.concatenate(pieces, axis=0)
    wide = jnp.concatenate([tall, jnp.zeros((72, T * HID - HID), jnp.float32)], axis=1)
    state = (lax.broadcasted_iota(jnp.int32, (72, T * HID), 0) % TL) // 2
    total = jnp.where(state == 0, wide, 0.0)
    for t in range(1, T):
        total = total + jnp.where(state == t, pltpu.roll(wide, t * HID, 1), 0.0)
    w2[...] = total.astype(jnp.bfloat16)


def build_guide(count, obs_step, obs_row, obs_col, obs_value, guide):
    slot = lax.broadcasted_iota(jnp.int32, (1, SLOTS), 1)
    live = slot < count[...]
    cell = jnp.where(live, obs_row[...] * TL + obs_step[...] * LAYERS, -1)
    hot = lax.broadcasted_iota(jnp.int32, (ROWS * TL, SLOTS), 0) == cell
    high, mid, low = three_parts(obs_value[...])
    left = jnp.concatenate(
        [
            jnp.where(hot, 1.0, 0.0),
            jnp.where(hot, high, 0.0),
            jnp.where(hot, mid, 0.0),
            jnp.where(hot, low, 0.0),
        ],
        axis=0,
    ).astype(jnp.bfloat16)
    right = jnp.where(
        lax.broadcasted_iota(jnp.int32, (COLS, SLOTS), 0) == obs_col[...], 1.0, 0.0
    ).astype(jnp.bfloat16)
    found = lax.dot_general(left, right, (((1,), (1,)), ((), ())), preferred_element_type=jnp.float32)
    rows = ROWS * TL
    guide[0:rows, :] = found[0:rows]
    guide[rows : 2 * rows, :] = (
        found[rows : 2 * rows] + found[2 * rows : 3 * rows] + found[3 * rows : 4 * rows]
    )


def kernel(
    sizes,
    x_hbm,
    first_hbm,
    second_hbm,
    w1_hbm,
    w2_hbm,
    embed_hbm,
    count_hbm,
    step_hbm,
    row_hbm,
    col_hbm,
    value_hbm,
    out,
    x_in,
    first,
    second,
    w1_raw,
    w2_raw,
    embed_raw,
    count,
    obs_step,
    obs_row,
    obs_col,
    obs_value,
    state,
    w1,
    w2,
    guide,
    tiles,
    frames,
    taps,
    load_sems,
    send_sems,
    recv_sems,
):
    n_tm, n_rows = sizes
    tm = lax.axis_index("tm")
    rw = lax.axis_index("rows")

    def peer(dt, dr):
        return {
            "tm": lax.rem(tm + dt + n_tm, n_tm) if dt else tm,
            "rows": lax.rem(rw + dr + n_rows, n_rows) if dr else rw,
        }

    barrier = pltpu.get_barrier_semaphore()
    for dt, dr in SENDS:
        pl.semaphore_signal(barrier, inc=1, device_id=peer(dt, dr), device_id_type=MESH)

    loads = [
        pltpu.make_async_copy(src, dst, load_sems.at[i])
        for i, (src, dst) in enumerate(
            (
                (x_hbm, x_in),
                (w1_hbm, w1_raw),
                (embed_hbm, embed_raw),
                (w2_hbm, w2_raw),
                (count_hbm, count),
                (step_hbm, obs_step),
                (row_hbm, obs_row),
                (col_hbm, obs_col),
                (value_hbm, obs_value),
                (first_hbm, first),
                (second_hbm, second),
            )
        )
    ]
    for load in loads:
        load.start()

    def send(index):
        copies = []
        for k, (dt, dr) in enumerate(SENDS):
            source = {0: slice(1, 5), 1: slice(4, 5), -1: slice(1, 2)}[dr]
            target = {0: slice(1, 5), 1: slice(0, 1), -1: slice(5, 6)}[dr]
            copies.append(
                pltpu.make_async_remote_copy(
                    src_ref=tiles.at[index, 1, source],
                    dst_ref=tiles.at[index, 1 - dt, target],
                    send_sem=send_sems.at[index, k],
                    recv_sem=recv_sems.at[index, k],
                    device_id=peer(dt, dr),
                    device_id_type=MESH,
                )
            )
        for copy in copies:
            copy.start()
        return copies

    def put_tiles(index, pair, upper, lower):
        scale = 1.0 / (1.0 + LEVELS[index] ** 2) ** 0.5
        tile = jnp.concatenate([upper, lower], axis=0) * scale
        tiles[index, 1, pair + 1] = tile.astype(jnp.bfloat16)

    def unpack(index, pair, block):
        tile = tiles[index, block, pair].astype(jnp.float32)
        if block == 0:
            tile = jnp.where(tm == 0, 0.0, tile)
        if block == 2:
            tile = jnp.where(tm == n_tm - 1, 0.0, tile)
        for b in range(3):
            moved = pltpu.roll(tile, (1 - b) % COLS, 1) if b != 1 else tile
            for half in range(2):
                at = (2 * pair + half) * 72 + b * 24 + block * 8
                frames[at : at + 8, :] = moved[half * 8 : half * 8 + 8]

    def hidden_band(index, j):
        window = frames[pl.ds(pl.multiple_of(72 * j, 8), 216), :]
        ones = jnp.full((K_IN - 216, COLS), LEVELS[index], jnp.float32)
        window = jnp.concatenate([window, ones], axis=0).astype(jnp.bfloat16)
        half = jnp.dot(w1[...], window, preferred_element_type=jnp.float32)
        hidden = (half + half * jnp.tanh(half)).astype(jnp.bfloat16)
        taps[j] = jnp.dot(w2[...], hidden, preferred_element_type=jnp.float32)

    def finish_row(index, r, noise):
        level_now, level_next = LEVELS[index], LEVELS[index + 1]
        sums = []
        for b in range(3):
            at = b * 24
            sums.append(
                taps[r, at : at + 8, :] + taps[r + 1, at + 8 : at + 16, :] + taps[r + 2, at + 16 : at + 24, :]
            )
        net = sums[1] + pltpu.roll(sums[0], 1, 1) + pltpu.roll(sums[2], COLS - 1, 1)
        current = state[r]
        base = 1.0 + level_now**2
        denoised = current * (1.0 / base) + (level_now / base**0.5) * net
        hits = guide[r * 8 : r * 8 + 8, :]
        values = guide[64 + r * 8 : 64 + r * 8 + 8, :]
        misfit = (values - hits * denoised) * (1.0 / (OBS_NOISE + COVARIANCE_GAIN * level_now**2))
        score = (denoised - current) * (1.0 / level_now**2) + misfit
        spread = level_now**2 - level_next**2
        return current + spread * score + spread**0.5 * noise[r]

    loads[0].wait()
    state[...] = jnp.swapaxes(x_in[...].reshape(TL, ROWS, COLS), 0, 1)
    for pair in range(4):
        put_tiles(0, pair, state[2 * pair], state[2 * pair + 1])
    pl.semaphore_wait(barrier, len(SENDS))
    copies = send(0)

    for load in loads[1:4]:
        load.wait()
    build_conv_in(w1_raw, embed_raw, w1)
    build_conv_out(w2_raw, w2)
    for load in loads[4:]:
        load.wait()
    build_guide(count, obs_step, obs_row, obs_col, obs_value, guide)
    turned_first = jnp.swapaxes(first[...].reshape(TL, ROWS, COLS), 0, 1)
    turned_second = jnp.swapaxes(second[...].reshape(TL, ROWS, COLS), 0, 1)

    for index in range(2):
        for pair in range(1, 5):
            unpack(index, pair, 1)
        for copy in copies:
            copy.wait_recv()
        for pair in range(1, 5):
            unpack(index, pair, 0)
            unpack(index, pair, 2)
        for block in range(3):
            unpack(index, 0, block)
            unpack(index, 5, block)

        def band(j, carry):
            hidden_band(index, j)
            return carry

        lax.fori_loop(0, BANDS, band, 0)
        for copy in copies:
            copy.wait_send()
        if index == 0:
            for pair in range(4):
                slabs = [finish_row(index, 2 * pair + half, turned_first) for half in range(2)]
                for half in range(2):
                    state[2 * pair + half] = slabs[half]
                put_tiles(1, pair, *slabs)
            copies = send(1)
        else:
            done = jnp.stack([finish_row(index, r, turned_second) for r in range(ROWS)], axis=0)
            out[...] = jnp.swapaxes(done, 0, 1).reshape(TL * ROWS, COLS)


def per_device(
    sizes,
    noisy_states,
    noise_first,
    noise_second,
    conv_in,
    conv_out,
    level_embed,
    obs_count,
    obs_step,
    obs_row,
    obs_col,
    obs_value,
):
    flat = (TL * ROWS, COLS)
    slots = (1, SLOTS)
    any_space = pl.BlockSpec(memory_space=pl.ANY)
    result = pl.pallas_call(
        functools.partial(kernel, sizes),
        out_shape=jax.ShapeDtypeStruct(flat, jnp.float32),
        in_specs=[any_space] * 11,
        out_specs=pl.BlockSpec(memory_space=pltpu.VMEM),
        scratch_shapes=[
            pltpu.VMEM(flat, jnp.float32),
            pltpu.VMEM(flat, jnp.float32),
            pltpu.VMEM(flat, jnp.float32),
            pltpu.VMEM((9, HID, C_IN), jnp.bfloat16),
            pltpu.VMEM((9, LAYERS, HID), jnp.bfloat16),
            pltpu.VMEM((1, HID), jnp.float32),
            pltpu.VMEM((1, 1), jnp.int32),
            pltpu.VMEM(slots, jnp.int32),
            pltpu.VMEM(slots, jnp.int32),
            pltpu.VMEM(slots, jnp.int32),
            pltpu.VMEM(slots, jnp.float32),
            pltpu.VMEM((ROWS, TL, COLS), jnp.float32),
            pltpu.VMEM((T * HID, K_IN), jnp.bfloat16),
            pltpu.VMEM((72, T * HID), jnp.bfloat16),
            pltpu.VMEM((2 * ROWS * TL, COLS), jnp.float32),
            pltpu.VMEM((2, 3, PAIRS, 16, COLS), jnp.bfloat16),
            pltpu.VMEM((2 * PAIRS * 72, COLS), jnp.float32),
            pltpu.VMEM((BANDS, 72, COLS), jnp.float32),
            pltpu.SemaphoreType.DMA((11,)),
            pltpu.SemaphoreType.DMA((2, len(SENDS))),
            pltpu.SemaphoreType.DMA((2, len(SENDS))),
        ],
        compiler_params=pltpu.CompilerParams(
            collective_id=0, has_side_effects=True, vmem_limit_bytes=32 * 1024 * 1024
        ),
        name="reverse_steps",
    )(
        noisy_states.reshape(flat),
        noise_first.reshape(flat),
        noise_second.reshape(flat),
        conv_in,
        conv_out,
        level_embed.reshape(1, HID),
        obs_count,
        obs_step.reshape(slots),
        obs_row.reshape(slots),
        obs_col.reshape(slots),
        obs_value.reshape(slots),
    )
    return result.reshape(noisy_states.shape)


def solution(mesh):
    sizes = (mesh.shape["tm"], mesh.shape["rows"])
    cells = P("tm", None, "rows", None)
    block = P("tm", "rows", None)
    return jax.shard_map(
        functools.partial(per_device, sizes),
        mesh=mesh,
        in_specs=(cells, cells, cells, P(), P(), P(), P("tm", "rows"), block, block, block, block),
        out_specs=cells,
        check_vma=False,
    )
```

```python
import functools

import jax
import jax.numpy as jnp
from jax import lax
from jax.experimental import pallas as pl
from jax.experimental.pallas import tpu as pltpu
from jax.sharding import PartitionSpec as P

MESH = pl.DeviceIdType.MESH
LEVELS = (1.0, 0.5, 0.2)
OBS_NOISE = 0.1
COVARIANCE_GAIN = 0.5
T = 4
LAYERS = 2
TL = 8
ROWS = 8
COLS = 256
HID = 96
C_IN = 18
SLOTS = 256
PAIRS = 6
BANDS = 10
K_IN = 224
NEIGHBOURS = ((0, -1), (0, 1), (-1, -1), (1, -1), (-1, 1), (1, 1), (-1, 0), (1, 0))
SLOT_OF = (0, 1, 4, 5, 2, 3)
ROWS_SENDS = tuple(
    (dt, dr, slice(1, 2) if dr < 0 else slice(2, 3), slice(3, 4) if dr < 0 else slice(0, 1))
    for dt, dr in NEIGHBOURS[:6]
)
EDGE_SENDS = tuple((dt, 0, slice(1, 3), slice(1, 3)) for dt in (-1, 1))
MID_SENDS = tuple((dt, 0, slice(4, 6), slice(4, 6)) for dt in (-1, 1))
SENDS = ROWS_SENDS + EDGE_SENDS + MID_SENDS
INNER_BANDS = (4, 5, 2, 3, 6, 7)
OUTER_BANDS = (0, 1, 8, 9)


def three_parts(values):
    high = values.astype(jnp.bfloat16).astype(jnp.float32)
    rest = values - high
    mid = rest.astype(jnp.bfloat16).astype(jnp.float32)
    return high, mid, rest - mid


def build_conv_in(w1_raw, embed_raw, w1_turned, w1):
    w1_turned[...] = jnp.zeros(w1_turned.shape, jnp.float32)
    for off in range(9):
        w1_turned[24 * off : 24 * off + C_IN, 0:HID] = w1_raw[off].astype(jnp.float32) * 0.5
    parts = three_parts(embed_raw[...] * 0.5)
    for piece in range(3):
        w1_turned[216 + piece : 217 + piece, 0:HID] = parts[piece]
    base = jnp.transpose(w1_turned[...])[:HID]
    lane = lax.broadcasted_iota(jnp.int32, (HID, 256), 1)
    for t in range(T):
        shifted = jnp.where(lane < 216, pltpu.roll(base, 2 * t, 1), base) if t else base
        w1[t * HID : (t + 1) * HID, :] = shifted[:, :K_IN].astype(jnp.bfloat16)


def build_conv_out(w2_raw, w2):
    sub = lax.broadcasted_iota(jnp.int32, (TL, HID), 0)
    pieces = []
    for b in range(3):
        for a in range(3):
            taps = w2_raw[3 * a + b].astype(jnp.float32)
            pieces.append(
                jnp.where(
                    sub % 2 == 0,
                    jnp.broadcast_to(taps[0:1], (TL, HID)),
                    jnp.broadcast_to(taps[1:2], (TL, HID)),
                )
            )
    tall = jnp.concatenate(pieces, axis=0)
    wide = jnp.concatenate([tall, jnp.zeros((72, T * HID - HID), jnp.float32)], axis=1)
    state = (lax.broadcasted_iota(jnp.int32, (72, T * HID), 0) % TL) // 2
    total = jnp.where(state == 0, wide, 0.0)
    for t in range(1, T):
        total = total + jnp.where(state == t, pltpu.roll(wide, t * HID, 1), 0.0)
    w2[...] = total.astype(jnp.bfloat16)


def build_guide(count, obs_step, obs_row, obs_col, obs_value, guide):
    slot = lax.broadcasted_iota(jnp.int32, (1, SLOTS), 1)
    live = slot < count[0, 0]
    cell = jnp.where(live, obs_row[...] * TL + obs_step[...] * LAYERS, -1)
    hot = lax.broadcasted_iota(jnp.int32, (ROWS * TL, SLOTS), 0) == cell
    high, mid, low = three_parts(obs_value[...])
    left = jnp.concatenate(
        [
            jnp.where(hot, 1.0, 0.0),
            jnp.where(hot, high, 0.0),
            jnp.where(hot, mid, 0.0),
            jnp.where(hot, low, 0.0),
        ],
        axis=0,
    ).astype(jnp.bfloat16)
    right = jnp.where(
        lax.broadcasted_iota(jnp.int32, (COLS, SLOTS), 0) == obs_col[...], 1.0, 0.0
    ).astype(jnp.bfloat16)
    found = lax.dot_general(left, right, (((1,), (1,)), ((), ())), preferred_element_type=jnp.float32)
    rows = ROWS * TL
    guide[0:rows, :] = found[0:rows]
    guide[rows : 2 * rows, :] = (
        found[rows : 2 * rows] + found[2 * rows : 3 * rows] + found[3 * rows : 4 * rows]
    )


def kernel(
    sizes,
    x_hbm,
    first_hbm,
    second_hbm,
    w1_hbm,
    w2_hbm,
    embed_hbm,
    count,
    step_hbm,
    row_hbm,
    col_hbm,
    value_hbm,
    out,
    x_in,
    first,
    second,
    w1_raw,
    w2_raw,
    embed_raw,
    obs_step,
    obs_row,
    obs_col,
    obs_value,
    state,
    turned_first,
    turned_second,
    w1_turned,
    w1,
    w2,
    guide,
    tiles,
    frames,
    taps,
    load_sems,
    send_sems,
    recv_sems,
):
    n_tm, n_rows = sizes
    tm = lax.axis_index("tm")
    rw = lax.axis_index("rows")

    def peer(dt, dr):
        return {
            "tm": lax.rem(tm + dt + n_tm, n_tm) if dt else tm,
            "rows": lax.rem(rw + dr + n_rows, n_rows) if dr else rw,
        }

    barrier = pltpu.get_barrier_semaphore()
    for dt, dr in NEIGHBOURS:
        pl.semaphore_signal(barrier, inc=1, device_id=peer(dt, dr), device_id_type=MESH)

    loads = [
        pltpu.make_async_copy(src, dst, load_sems.at[i])
        for i, (src, dst) in enumerate(
            (
                (x_hbm, x_in),
                (w1_hbm, w1_raw),
                (embed_hbm, embed_raw),
                (w2_hbm, w2_raw),
                (step_hbm, obs_step),
                (row_hbm, obs_row),
                (col_hbm, obs_col),
                (value_hbm, obs_value),
                (first_hbm, first),
                (second_hbm, second),
            )
        )
    ]
    for load in loads:
        load.start()

    copies = [
        [
            pltpu.make_async_remote_copy(
                src_ref=tiles.at[index, 1, source],
                dst_ref=tiles.at[index, 1 - dt, target],
                send_sem=send_sems.at[index, k],
                recv_sem=recv_sems.at[index, k],
                device_id=peer(dt, dr),
                device_id_type=MESH,
            )
            for k, (dt, dr, source, target) in enumerate(SENDS)
        ]
        for index in range(2)
    ]

    def put_tiles(index, pair, upper, lower):
        scale = 1.0 / (1.0 + LEVELS[index] ** 2) ** 0.5
        tile = jnp.concatenate([upper, lower], axis=0) * scale
        tiles[index, 1, SLOT_OF[pair + 1]] = tile.astype(jnp.bfloat16)

    def unpack(index, pair, block):
        tile = tiles[index, block, SLOT_OF[pair]].astype(jnp.float32)
        if block == 0:
            tile = jnp.where(tm == 0, 0.0, tile)
        if block == 2:
            tile = jnp.where(tm == n_tm - 1, 0.0, tile)
        for b in range(3):
            moved = pltpu.roll(tile, (1 - b) % COLS, 1) if b != 1 else tile
            for half in range(2):
                at = (2 * pair + half) * 72 + b * 24 + block * 8
                frames[at : at + 8, :] = moved[half * 8 : half * 8 + 8]

    def hidden_band(index, j):
        ones = jnp.full((K_IN - 216, COLS), LEVELS[index], jnp.float32)
        window = jnp.concatenate([frames[72 * j : 72 * j + 216, :], ones], axis=0).astype(jnp.bfloat16)
        half = jnp.dot(w1[...], window, preferred_element_type=jnp.float32)
        hidden = (half + half * jnp.tanh(half)).astype(jnp.bfloat16)
        taps[j] = jnp.dot(w2[...], hidden, preferred_element_type=jnp.float32)

    def finish_row(index, r, noise):
        level_now, level_next = LEVELS[index], LEVELS[index + 1]
        sums = []
        for b in range(3):
            at = b * 24
            sums.append(
                taps[r, at : at + 8, :] + taps[r + 1, at + 8 : at + 16, :] + taps[r + 2, at + 16 : at + 24, :]
            )
        net = sums[1] + pltpu.roll(sums[0], 1, 1) + pltpu.roll(sums[2], COLS - 1, 1)
        current = state[r]
        base = 1.0 + level_now**2
        denoised = current * (1.0 / base) + (level_now / base**0.5) * net
        hits = guide[r * 8 : r * 8 + 8, :]
        values = guide[64 + r * 8 : 64 + r * 8 + 8, :]
        misfit = (values - hits * denoised) * (1.0 / (OBS_NOISE + COVARIANCE_GAIN * level_now**2))
        score = (denoised - current) * (1.0 / level_now**2) + misfit
        spread = level_now**2 - level_next**2
        return current + spread * score + spread**0.5 * noise[r]

    def step_pair(pair):
        slabs = [finish_row(0, 2 * pair + half, turned_first) for half in range(2)]
        put_tiles(1, pair, *slabs)
        for half in range(2):
            state[2 * pair + half] = slabs[half]

    n_rows_sends = len(ROWS_SENDS)

    def exchange_inner(index):
        for pair in range(1, 5):
            unpack(index, pair, 1)
        for copy in copies[index][n_rows_sends:]:
            copy.wait_recv()
        for pair in range(1, 5):
            unpack(index, pair, 0)
            unpack(index, pair, 2)

    def exchange_outer(index):
        for copy in copies[index][:n_rows_sends]:
            copy.wait_recv()
        for block in range(3):
            unpack(index, 0, block)
            unpack(index, 5, block)

    loads[0].wait()
    state[...] = jnp.swapaxes(x_in[...].reshape(TL, ROWS, COLS), 0, 1)
    for pair in range(4):
        put_tiles(0, pair, state[2 * pair], state[2 * pair + 1])
    for load in loads[1:4]:
        load.wait()
    build_conv_in(w1_raw, embed_raw, w1_turned, w1)
    build_conv_out(w2_raw, w2)
    pl.semaphore_wait(barrier, len(NEIGHBOURS))
    for copy in copies[0]:
        copy.start()
    for load in loads[4:]:
        load.wait()
    build_guide(count, obs_step, obs_row, obs_col, obs_value, guide)
    turned_first[...] = jnp.swapaxes(first[...].reshape(TL, ROWS, COLS), 0, 1)
    turned_second[...] = jnp.swapaxes(second[...].reshape(TL, ROWS, COLS), 0, 1)

    exchange_inner(0)
    for j in INNER_BANDS:
        hidden_band(0, j)
    for pair in (1, 2):
        step_pair(pair)
    for copy in copies[1][n_rows_sends + 2 :]:
        copy.start()
    exchange_outer(0)
    for j in OUTER_BANDS:
        hidden_band(0, j)
    for pair in (0, 3):
        step_pair(pair)
    for copy in copies[1][: n_rows_sends + 2]:
        copy.start()

    exchange_inner(1)
    for j in INNER_BANDS:
        hidden_band(1, j)
    exchange_outer(1)
    for j in OUTER_BANDS:
        hidden_band(1, j)
    done = jnp.stack([finish_row(1, r, turned_second) for r in range(ROWS)], axis=0)
    out[...] = jnp.swapaxes(done, 0, 1).reshape(TL * ROWS, COLS)
    for index in range(2):
        for copy in copies[index]:
            copy.wait_send()


def per_device(
    sizes,
    noisy_states,
    noise_first,
    noise_second,
    conv_in,
    conv_out,
    level_embed,
    obs_count,
    obs_step,
    obs_row,
    obs_col,
    obs_value,
):
    flat = (TL * ROWS, COLS)
    slots = (1, SLOTS)
    far = pl.BlockSpec(memory_space=pltpu.HBM)
    result = pl.pallas_call(
        functools.partial(kernel, sizes),
        out_shape=pltpu.VMEM(flat, jnp.float32),
        in_specs=[far] * 6 + [pl.BlockSpec(memory_space=pltpu.SMEM)] + [far] * 4,
        out_specs=pl.BlockSpec(memory_space=pltpu.VMEM),
        scratch_shapes=[
            pltpu.VMEM(flat, jnp.float32),
            pltpu.VMEM(flat, jnp.float32),
            pltpu.VMEM(flat, jnp.float32),
            pltpu.VMEM((9, C_IN, HID), jnp.bfloat16),
            pltpu.VMEM((9, LAYERS, HID), jnp.bfloat16),
            pltpu.VMEM((1, HID), jnp.float32),
            pltpu.VMEM(slots, jnp.int32),
            pltpu.VMEM(slots, jnp.int32),
            pltpu.VMEM(slots, jnp.int32),
            pltpu.VMEM(slots, jnp.float32),
            pltpu.VMEM((ROWS, TL, COLS), jnp.float32),
            pltpu.VMEM((ROWS, TL, COLS), jnp.float32),
            pltpu.VMEM((ROWS, TL, COLS), jnp.float32),
            pltpu.VMEM((256, 128), jnp.float32),
            pltpu.VMEM((T * HID, K_IN), jnp.bfloat16),
            pltpu.VMEM((72, T * HID), jnp.bfloat16),
            pltpu.VMEM((2 * ROWS * TL, COLS), jnp.float32),
            pltpu.VMEM((2, 3, PAIRS, 16, COLS), jnp.bfloat16),
            pltpu.VMEM((2 * PAIRS * 72, COLS), jnp.float32),
            pltpu.VMEM((BANDS, 72, COLS), jnp.float32),
            pltpu.SemaphoreType.DMA((10,)),
            pltpu.SemaphoreType.DMA((2, len(SENDS))),
            pltpu.SemaphoreType.DMA((2, len(SENDS))),
        ],
        compiler_params=pltpu.CompilerParams(
            collective_id=0, has_side_effects=True, vmem_limit_bytes=32 * 1024 * 1024
        ),
        name="reverse_steps",
    )(
        *(
            operand if operand is obs_count else pltpu.with_memory_space_constraint(operand, pltpu.HBM)
            for operand in (
                noisy_states.reshape(flat),
                noise_first.reshape(flat),
                noise_second.reshape(flat),
                jnp.swapaxes(conv_in, 1, 2),
                conv_out,
                level_embed.reshape(1, HID),
                obs_count,
                obs_step.reshape(slots),
                obs_row.reshape(slots),
                obs_col.reshape(slots),
                obs_value.reshape(slots),
            )
        )
    )
    return result.reshape(noisy_states.shape)


def solution(mesh):
    sizes = (mesh.shape["tm"], mesh.shape["rows"])
    cells = P("tm", None, "rows", None)
    block = P("tm", "rows", None)
    return jax.shard_map(
        functools.partial(per_device, sizes),
        mesh=mesh,
        in_specs=(cells, cells, cells, P(), P(), P(), P("tm", "rows"), block, block, block, block),
        out_specs=cells,
        check_vma=False,
    )
```

```python
import functools

import jax
import jax.numpy as jnp
from jax import lax
from jax.experimental import pallas as pl
from jax.experimental.pallas import tpu as pltpu
from jax.sharding import PartitionSpec as P

MESH = pl.DeviceIdType.MESH
LEVELS = (1.0, 0.5, 0.2)
OBS_NOISE = 0.1
COVARIANCE_GAIN = 0.5
T = 4
LAYERS = 2
TL = 8
ROWS = 8
COLS = 256
HID = 96
C_IN = 18
SLOTS = 256
PAIRS = 8
BANDS = 14
K_IN = 224
NEIGHBOURS = ((0, -1), (0, 1), (-1, -1), (1, -1), (-1, 1), (1, 1), (-1, 0), (1, 0))
TOP, MID, BOTTOM = slice(1, 3), slice(3, 5), slice(5, 7)
FIRST_SENDS = tuple(
    (dt, dr, *{-1: (slice(2, 4), slice(6, 8)), 1: (slice(4, 6), slice(0, 2)), 0: (slice(2, 6), slice(2, 6))}[dr])
    for dt, dr in NEIGHBOURS
)
SECOND_SENDS = tuple((dt, 0, part, part) for part in (MID, TOP, BOTTOM) for dt in (-1, 1))


def three_parts(values):
    high = values.astype(jnp.bfloat16).astype(jnp.float32)
    rest = values - high
    mid = rest.astype(jnp.bfloat16).astype(jnp.float32)
    return high, mid, rest - mid


def build_conv_in(w1_raw, embed_raw, w1_turned, w1):
    w1_turned[...] = jnp.zeros(w1_turned.shape, jnp.float32)
    for off in range(9):
        w1_turned[24 * off : 24 * off + C_IN, 0:HID] = w1_raw[off].astype(jnp.float32) * 0.5
    parts = three_parts(embed_raw[...] * 0.5)
    for piece in range(3):
        w1_turned[216 + piece : 217 + piece, 0:HID] = parts[piece]
    base = jnp.transpose(w1_turned[...])[:HID]
    lane = lax.broadcasted_iota(jnp.int32, (HID, 256), 1)
    for t in range(T):
        shifted = jnp.where(lane < 216, pltpu.roll(base, 2 * t, 1), base) if t else base
        w1[t * HID : (t + 1) * HID, :] = shifted[:, :K_IN].astype(jnp.bfloat16)


def build_conv_out(w2_raw, w2):
    sub = lax.broadcasted_iota(jnp.int32, (TL, HID), 0)
    pieces = []
    for b in range(3):
        for a in range(3):
            taps = w2_raw[3 * a + b].astype(jnp.float32)
            pieces.append(
                jnp.where(
                    sub % 2 == 0,
                    jnp.broadcast_to(taps[0:1], (TL, HID)),
                    jnp.broadcast_to(taps[1:2], (TL, HID)),
                )
            )
    tall = jnp.concatenate(pieces, axis=0)
    wide = jnp.concatenate([tall, jnp.zeros((72, T * HID - HID), jnp.float32)], axis=1)
    state = (lax.broadcasted_iota(jnp.int32, (72, T * HID), 0) % TL) // 2
    total = jnp.where(state == 0, wide, 0.0)
    for t in range(1, T):
        total = total + jnp.where(state == t, pltpu.roll(wide, t * HID, 1), 0.0)
    w2[...] = total.astype(jnp.bfloat16)


def build_guide(count, obs_step, obs_row, obs_col, obs_value, guide):
    slot = lax.broadcasted_iota(jnp.int32, (1, SLOTS), 1)
    live = slot < count[0, 0]
    cell = jnp.where(live, obs_row[...] * TL + obs_step[...] * LAYERS, -1)
    hot = lax.broadcasted_iota(jnp.int32, (ROWS * TL, SLOTS), 0) == cell
    high, mid, low = three_parts(obs_value[...])
    left = jnp.concatenate(
        [
            jnp.where(hot, 1.0, 0.0),
            jnp.where(hot, high, 0.0),
            jnp.where(hot, mid, 0.0),
            jnp.where(hot, low, 0.0),
        ],
        axis=0,
    ).astype(jnp.bfloat16)
    right = jnp.where(
        lax.broadcasted_iota(jnp.int32, (COLS, SLOTS), 0) == obs_col[...], 1.0, 0.0
    ).astype(jnp.bfloat16)
    found = lax.dot_general(left, right, (((1,), (1,)), ((), ())), preferred_element_type=jnp.float32)
    rows = ROWS * TL
    guide[0:rows, :] = found[0:rows]
    guide[rows : 2 * rows, :] = (
        found[rows : 2 * rows] + found[2 * rows : 3 * rows] + found[3 * rows : 4 * rows]
    )


def kernel(
    sizes,
    x_hbm,
    first_hbm,
    second_hbm,
    w1_hbm,
    w2_hbm,
    embed_hbm,
    count,
    step_hbm,
    row_hbm,
    col_hbm,
    value_hbm,
    out,
    x_in,
    first,
    second,
    w1_raw,
    w2_raw,
    embed_raw,
    obs_step,
    obs_row,
    obs_col,
    obs_value,
    state,
    turned_second,
    affine,
    w1_turned,
    w1,
    w2,
    guide,
    tiles,
    frames,
    taps,
    load_sems,
    send_sems,
    recv_sems,
):
    n_tm, n_rows = sizes
    tm = lax.axis_index("tm")
    rw = lax.axis_index("rows")

    def peer(dt, dr):
        return {
            "tm": lax.rem(tm + dt + n_tm, n_tm) if dt else tm,
            "rows": lax.rem(rw + dr + n_rows, n_rows) if dr else rw,
        }

    barrier = pltpu.get_barrier_semaphore()
    for dt, dr in NEIGHBOURS:
        pl.semaphore_signal(barrier, inc=1, device_id=peer(dt, dr), device_id_type=MESH)

    loads = [
        pltpu.make_async_copy(src, dst, load_sems.at[i])
        for i, (src, dst) in enumerate(
            (
                (x_hbm, x_in),
                (step_hbm, obs_step),
                (row_hbm, obs_row),
                (col_hbm, obs_col),
                (value_hbm, obs_value),
                (first_hbm, first),
                (w1_hbm, w1_raw),
                (embed_hbm, embed_raw),
                (w2_hbm, w2_raw),
                (second_hbm, second),
            )
        )
    ]
    for load in loads:
        load.start()

    def copies_of(index, sends):
        return [
            pltpu.make_async_remote_copy(
                src_ref=tiles.at[index, 1, source],
                dst_ref=tiles.at[index, 1 - dt, target],
                send_sem=send_sems.at[index, k],
                recv_sem=recv_sems.at[index, k],
                device_id=peer(dt, dr),
                device_id_type=MESH,
            )
            for k, (dt, dr, source, target) in enumerate(sends)
        ]

    first_copies = copies_of(0, FIRST_SENDS)
    second_copies = copies_of(1, SECOND_SENDS)
    affine_copies = [
        pltpu.make_async_remote_copy(
            src_ref=affine.at[source],
            dst_ref=affine.at[target],
            send_sem=send_sems.at[2, k],
            recv_sem=recv_sems.at[2, k],
            device_id=peer(0, dr),
            device_id_type=MESH,
        )
        for k, (dr, source, target) in enumerate(
            ((-1, slice(2, 4), slice(10, 12)), (1, slice(8, 10), slice(0, 2)))
        )
    ]

    def put_tiles(index, pair, upper, lower):
        scale = 1.0 / (1.0 + LEVELS[index] ** 2) ** 0.5
        tile = jnp.concatenate([upper, lower], axis=0) * scale
        tiles[index, 1, pair] = tile.astype(jnp.bfloat16)

    def unpack(index, pair, block):
        tile = tiles[index, block, pair].astype(jnp.float32)
        if block == 0:
            tile = jnp.where(tm == 0, 0.0, tile)
        if block == 2:
            tile = jnp.where(tm == n_tm - 1, 0.0, tile)
        for b in range(3):
            moved = pltpu.roll(tile, (1 - b) % COLS, 1) if b != 1 else tile
            for half in range(2):
                at = (2 * pair + half) * 72 + b * 24 + block * 8
                frames[at : at + 8, :] = moved[half * 8 : half * 8 + 8]

    def hidden_band(index, j):
        ones = jnp.full((K_IN - 216, COLS), LEVELS[index], jnp.float32)
        window = jnp.concatenate([frames[72 * j : 72 * j + 216, :], ones], axis=0).astype(jnp.bfloat16)
        half = jnp.dot(w1[...], window, preferred_element_type=jnp.float32)
        hidden = (half + half * jnp.tanh(half)).astype(jnp.bfloat16)
        taps[j] = jnp.dot(w2[...], hidden, preferred_element_type=jnp.float32)

    def affine_row(index, r, current, noise):
        level_now, level_next = LEVELS[index], LEVELS[index + 1]
        base = 1.0 + level_now**2
        spread = level_now**2 - level_next**2
        keep = 1.0 / level_now**2
        gain = 1.0 / (OBS_NOISE + COVARIANCE_GAIN * level_now**2)
        hits = guide[r * 8 : r * 8 + 8, :]
        values = guide[64 + r * 8 : 64 + r * 8 + 8, :]
        still = current * (1.0 / base)
        score = (still - current) * keep + (values - hits * still) * gain
        shift = current + spread * score + spread**0.5 * noise
        slope = (spread * level_now / base**0.5) * (keep - gain * hits)
        return shift, slope

    def net_row(r):
        at = r
        sums = [
            taps[at, b * 24 : b * 24 + 8, :]
            + taps[at + 1, b * 24 + 8 : b * 24 + 16, :]
            + taps[at + 2, b * 24 + 16 : b * 24 + 24, :]
            for b in range(3)
        ]
        return sums[1] + pltpu.roll(sums[0], 1, 1) + pltpu.roll(sums[2], COLS - 1, 1)

    def step_pair(pair):
        slabs = []
        for half in range(2):
            r = 2 * (pair - 1) + half
            slabs.append(affine[r, 0:8, :] + affine[r, 8:16, :] * net_row(r))
        put_tiles(1, pair, *slabs)
        if 2 <= pair < 6:
            for half in range(2):
                state[2 * (pair - 2) + half] = slabs[half]

    def unpack_pairs(index, pairs, blocks):
        for pair in pairs:
            for block in blocks:
                unpack(index, pair, block)

    def bands(index, rows):
        for j in rows:
            hidden_band(index, j)

    loads[0].wait()
    state[...] = jnp.swapaxes(x_in[...].reshape(TL, ROWS, COLS), 0, 1)
    for pair in range(4):
        put_tiles(0, pair + 2, state[2 * pair], state[2 * pair + 1])
    for load in loads[1:6]:
        load.wait()
    build_guide(count, obs_step, obs_row, obs_col, obs_value, guide)
    turned = jnp.swapaxes(first[...].reshape(TL, ROWS, COLS), 0, 1)
    for r in range(ROWS):
        shift, slope = affine_row(0, r, state[r], turned[r])
        affine[r + 2, 0:8, :] = shift
        affine[r + 2, 8:16, :] = slope
    pl.semaphore_wait(barrier, len(NEIGHBOURS))
    for copy in first_copies:
        copy.start()
    for copy in affine_copies:
        copy.start()
    for load in loads[6:]:
        load.wait()
    build_conv_in(w1_raw, embed_raw, w1_turned, w1)
    build_conv_out(w2_raw, w2)
    turned_second[...] = jnp.swapaxes(second[...].reshape(TL, ROWS, COLS), 0, 1)

    unpack_pairs(0, range(2, 6), (1,))
    for copy in first_copies[6:]:
        copy.wait_recv()
    unpack_pairs(0, range(2, 6), (0, 2))
    bands(0, range(4, 10))
    for pair in (3, 4):
        step_pair(pair)
    for copy in second_copies[:2]:
        copy.start()
    for copy in first_copies[:6]:
        copy.wait_recv()
    unpack_pairs(0, (0, 1, 6, 7), range(3))
    for copy in affine_copies:
        copy.wait_recv()
    bands(0, range(0, 4))
    for pair in (1, 2):
        step_pair(pair)
    for copy in second_copies[2:4]:
        copy.start()
    bands(0, range(10, 14))
    for pair in (5, 6):
        step_pair(pair)
    for copy in second_copies[4:]:
        copy.start()

    unpack_pairs(1, range(1, 7), (1,))
    for copy in second_copies:
        copy.wait_recv()
    unpack_pairs(1, range(1, 7), (0, 2))
    bands(1, range(2, 12))
    done = []
    for r in range(ROWS):
        shift, slope = affine_row(1, r, state[r], turned_second[r])
        done.append(shift + slope * net_row(r + 2))
    out[...] = jnp.swapaxes(jnp.stack(done, axis=0), 0, 1).reshape(TL * ROWS, COLS)
    for copy in (*first_copies, *affine_copies, *second_copies):
        copy.wait_send()


def per_device(
    sizes,
    noisy_states,
    noise_first,
    noise_second,
    conv_in,
    conv_out,
    level_embed,
    obs_count,
    obs_step,
    obs_row,
    obs_col,
    obs_value,
):
    flat = (TL * ROWS, COLS)
    slots = (1, SLOTS)
    far = pl.BlockSpec(memory_space=pltpu.HBM)
    result = pl.pallas_call(
        functools.partial(kernel, sizes),
        out_shape=pltpu.VMEM(flat, jnp.float32),
        in_specs=[far] * 6 + [pl.BlockSpec(memory_space=pltpu.SMEM)] + [far] * 4,
        out_specs=pl.BlockSpec(memory_space=pltpu.VMEM),
        scratch_shapes=[
            pltpu.VMEM(flat, jnp.float32),
            pltpu.VMEM(flat, jnp.float32),
            pltpu.VMEM(flat, jnp.float32),
            pltpu.VMEM((9, C_IN, HID), jnp.bfloat16),
            pltpu.VMEM((9, LAYERS, HID), jnp.bfloat16),
            pltpu.VMEM((1, HID), jnp.float32),
            pltpu.VMEM(slots, jnp.int32),
            pltpu.VMEM(slots, jnp.int32),
            pltpu.VMEM(slots, jnp.int32),
            pltpu.VMEM(slots, jnp.float32),
            pltpu.VMEM((ROWS, TL, COLS), jnp.float32),
            pltpu.VMEM((ROWS, TL, COLS), jnp.float32),
            pltpu.VMEM((ROWS + 4, 2 * TL, COLS), jnp.float32),
            pltpu.VMEM((256, 128), jnp.float32),
            pltpu.VMEM((T * HID, K_IN), jnp.bfloat16),
            pltpu.VMEM((72, T * HID), jnp.bfloat16),
            pltpu.VMEM((2 * ROWS * TL, COLS), jnp.float32),
            pltpu.VMEM((2, 3, PAIRS, 16, COLS), jnp.bfloat16),
            pltpu.VMEM((2 * PAIRS * 72, COLS), jnp.float32),
            pltpu.VMEM((BANDS, 72, COLS), jnp.float32),
            pltpu.SemaphoreType.DMA((10,)),
            pltpu.SemaphoreType.DMA((3, len(NEIGHBOURS))),
            pltpu.SemaphoreType.DMA((3, len(NEIGHBOURS))),
        ],
        compiler_params=pltpu.CompilerParams(
            collective_id=0, has_side_effects=True, vmem_limit_bytes=32 * 1024 * 1024
        ),
        name="reverse_steps",
    )(
        *(
            operand if operand is obs_count else pltpu.with_memory_space_constraint(operand, pltpu.HBM)
            for operand in (
                noisy_states.reshape(flat),
                noise_first.reshape(flat),
                noise_second.reshape(flat),
                jnp.swapaxes(conv_in, 1, 2),
                conv_out,
                level_embed.reshape(1, HID),
                obs_count,
                obs_step.reshape(slots),
                obs_row.reshape(slots),
                obs_col.reshape(slots),
                obs_value.reshape(slots),
            )
        )
    )
    return result.reshape(noisy_states.shape)


def solution(mesh):
    sizes = (mesh.shape["tm"], mesh.shape["rows"])
    cells = P("tm", None, "rows", None)
    block = P("tm", "rows", None)
    return jax.shard_map(
        functools.partial(per_device, sizes),
        mesh=mesh,
        in_specs=(cells, cells, cells, P(), P(), P(), P("tm", "rows"), block, block, block, block),
        out_specs=cells,
        check_vma=False,
    )
```

```python
import functools

import jax
import jax.numpy as jnp
from jax import lax
from jax.experimental import pallas as pl
from jax.experimental.pallas import tpu as pltpu
from jax.sharding import PartitionSpec as P

MESH = pl.DeviceIdType.MESH
LEVELS = (1.0, 0.5, 0.2)
OBS_NOISE = 0.1
COVARIANCE_GAIN = 0.5
T = 4
LAYERS = 2
TL = 8
ROWS = 8
COLS = 256
HID = 96
C_IN = 18
SLOTS = 256
PAIRS = 6
BANDS = 10
K_IN = 224
NEIGHBOURS = ((0, -1), (0, 1), (-1, -1), (1, -1), (-1, 1), (1, 1), (-1, 0), (1, 0))
SLOT_OF = (0, 1, 4, 5, 2, 3)
ROWS_SENDS = tuple(
    (dt, dr, slice(1, 2) if dr < 0 else slice(2, 3), slice(3, 4) if dr < 0 else slice(0, 1))
    for dt, dr in NEIGHBOURS[:6]
)
EDGE_SENDS = tuple((dt, 0, slice(1, 3), slice(1, 3)) for dt in (-1, 1))
MID_SENDS = tuple((dt, 0, slice(4, 6), slice(4, 6)) for dt in (-1, 1))
SENDS = ROWS_SENDS + EDGE_SENDS + MID_SENDS
INNER_BANDS = (4, 5, 2, 3, 6, 7)
OUTER_BANDS = (0, 1, 8, 9)


def three_parts(values):
    high = values.astype(jnp.bfloat16).astype(jnp.float32)
    rest = values - high
    mid = rest.astype(jnp.bfloat16).astype(jnp.float32)
    return high, mid, rest - mid


def build_conv_in(w1_raw, embed_raw, w1_turned, w1):
    w1_turned[...] = jnp.zeros(w1_turned.shape, jnp.float32)
    for off in range(9):
        w1_turned[24 * off : 24 * off + C_IN, 0:HID] = w1_raw[off].astype(jnp.float32) * 0.5
    parts = three_parts(embed_raw[...] * 0.5)
    for piece in range(3):
        w1_turned[216 + piece : 217 + piece, 0:HID] = parts[piece]
    base = jnp.transpose(w1_turned[...])[:HID]
    lane = lax.broadcasted_iota(jnp.int32, (HID, 256), 1)
    for t in range(T):
        shifted = jnp.where(lane < 216, pltpu.roll(base, 2 * t, 1), base) if t else base
        w1[t * HID : (t + 1) * HID, :] = shifted[:, :K_IN].astype(jnp.bfloat16)


def build_conv_out(w2_raw, w2):
    sub = lax.broadcasted_iota(jnp.int32, (TL, HID), 0)
    pieces = []
    for b in range(3):
        for a in range(3):
            taps = w2_raw[3 * a + b].astype(jnp.float32)
            pieces.append(
                jnp.where(
                    sub % 2 == 0,
                    jnp.broadcast_to(taps[0:1], (TL, HID)),
                    jnp.broadcast_to(taps[1:2], (TL, HID)),
                )
            )
    tall = jnp.concatenate(pieces, axis=0)
    wide = jnp.concatenate([tall, jnp.zeros((72, T * HID - HID), jnp.float32)], axis=1)
    state = (lax.broadcasted_iota(jnp.int32, (72, T * HID), 0) % TL) // 2
    total = jnp.where(state == 0, wide, 0.0)
    for t in range(1, T):
        total = total + jnp.where(state == t, pltpu.roll(wide, t * HID, 1), 0.0)
    w2[...] = total.astype(jnp.bfloat16)


def build_guide(count, obs_step, obs_row, obs_col, obs_value, guide):
    slot = lax.broadcasted_iota(jnp.int32, (1, SLOTS), 1)
    live = slot < count[0, 0]
    cell = jnp.where(live, obs_row[...] * TL + obs_step[...] * LAYERS, -1)
    hot = lax.broadcasted_iota(jnp.int32, (ROWS * TL, SLOTS), 0) == cell
    high, mid, low = three_parts(obs_value[...])
    left = jnp.concatenate(
        [
            jnp.where(hot, 1.0, 0.0),
            jnp.where(hot, high, 0.0),
            jnp.where(hot, mid, 0.0),
            jnp.where(hot, low, 0.0),
        ],
        axis=0,
    ).astype(jnp.bfloat16)
    right = jnp.where(
        lax.broadcasted_iota(jnp.int32, (COLS, SLOTS), 0) == obs_col[...], 1.0, 0.0
    ).astype(jnp.bfloat16)
    found = lax.dot_general(left, right, (((1,), (1,)), ((), ())), preferred_element_type=jnp.float32)
    rows = ROWS * TL
    guide[0:rows, :] = found[0:rows]
    guide[rows : 2 * rows, :] = (
        found[rows : 2 * rows] + found[2 * rows : 3 * rows] + found[3 * rows : 4 * rows]
    )


def kernel(
    sizes,
    x_hbm,
    first_hbm,
    second_hbm,
    w1_hbm,
    w2_hbm,
    embed_hbm,
    count,
    step_hbm,
    row_hbm,
    col_hbm,
    value_hbm,
    out,
    x_in,
    first,
    second,
    w1_raw,
    w2_raw,
    embed_raw,
    obs_step,
    obs_row,
    obs_col,
    obs_value,
    state,
    turned_first,
    turned_second,
    w1_turned,
    w1,
    w2,
    guide,
    tiles,
    frames,
    taps,
    load_sems,
    send_sems,
    recv_sems,
):
    n_tm, n_rows = sizes
    tm = lax.axis_index("tm")
    rw = lax.axis_index("rows")

    def peer(dt, dr):
        return {
            "tm": lax.rem(tm + dt + n_tm, n_tm) if dt else tm,
            "rows": lax.rem(rw + dr + n_rows, n_rows) if dr else rw,
        }

    barrier = pltpu.get_barrier_semaphore()
    for dt, dr in NEIGHBOURS:
        pl.semaphore_signal(barrier, inc=1, device_id=peer(dt, dr), device_id_type=MESH)

    loads = [
        pltpu.make_async_copy(src, dst, load_sems.at[i])
        for i, (src, dst) in enumerate(
            (
                (x_hbm, x_in),
                (w1_hbm, w1_raw),
                (embed_hbm, embed_raw),
                (w2_hbm, w2_raw),
                (step_hbm, obs_step),
                (row_hbm, obs_row),
                (col_hbm, obs_col),
                (value_hbm, obs_value),
                (first_hbm, first),
                (second_hbm, second),
            )
        )
    ]
    for load in loads:
        load.start()

    copies = [
        [
            pltpu.make_async_remote_copy(
                src_ref=tiles.at[index, 1, source],
                dst_ref=tiles.at[index, 1 - dt, target],
                send_sem=send_sems.at[index, k],
                recv_sem=recv_sems.at[index, k],
                device_id=peer(dt, dr),
                device_id_type=MESH,
            )
            for k, (dt, dr, source, target) in enumerate(SENDS)
        ]
        for index in range(2)
    ]

    def put_tiles(index, pair, upper, lower):
        scale = 1.0 / (1.0 + LEVELS[index] ** 2) ** 0.5
        tile = jnp.concatenate([upper, lower], axis=0) * scale
        tiles[index, 1, SLOT_OF[pair + 1]] = tile.astype(jnp.bfloat16)

    def unpack(index, pair, block):
        tile = tiles[index, block, SLOT_OF[pair]].astype(jnp.float32)
        if block == 0:
            tile = jnp.where(tm == 0, 0.0, tile)
        if block == 2:
            tile = jnp.where(tm == n_tm - 1, 0.0, tile)
        for b in range(3):
            moved = pltpu.roll(tile, (1 - b) % COLS, 1) if b != 1 else tile
            for half in range(2):
                at = (2 * pair + half) * 72 + b * 24 + block * 8
                frames[at : at + 8, :] = moved[half * 8 : half * 8 + 8]

    def hidden_bands(index, group):
        ones = jnp.full((K_IN - 216, COLS), LEVELS[index], jnp.float32)
        windows = jnp.concatenate(
            [
                jnp.concatenate([frames[72 * j : 72 * j + 216, :], ones], axis=0).astype(jnp.bfloat16)
                for j in group
            ],
            axis=1,
        )
        half = jnp.dot(w1[...], windows, preferred_element_type=jnp.float32)
        hidden = (half + half * jnp.tanh(half)).astype(jnp.bfloat16)
        found = jnp.dot(w2[...], hidden, preferred_element_type=jnp.float32)
        for k, j in enumerate(group):
            taps[j] = found[:, k * COLS : (k + 1) * COLS]

    def finish_row(index, r, noise):
        level_now, level_next = LEVELS[index], LEVELS[index + 1]
        sums = []
        for b in range(3):
            at = b * 24
            sums.append(
                taps[r, at : at + 8, :] + taps[r + 1, at + 8 : at + 16, :] + taps[r + 2, at + 16 : at + 24, :]
            )
        net = sums[1] + pltpu.roll(sums[0], 1, 1) + pltpu.roll(sums[2], COLS - 1, 1)
        current = state[r]
        base = 1.0 + level_now**2
        denoised = current * (1.0 / base) + (level_now / base**0.5) * net
        hits = guide[r * 8 : r * 8 + 8, :]
        values = guide[64 + r * 8 : 64 + r * 8 + 8, :]
        misfit = (values - hits * denoised) * (1.0 / (OBS_NOISE + COVARIANCE_GAIN * level_now**2))
        score = (denoised - current) * (1.0 / level_now**2) + misfit
        spread = level_now**2 - level_next**2
        return current + spread * score + spread**0.5 * noise[r]

    def step_pair(pair):
        slabs = [finish_row(0, 2 * pair + half, turned_first) for half in range(2)]
        put_tiles(1, pair, *slabs)
        for half in range(2):
            state[2 * pair + half] = slabs[half]

    n_rows_sends = len(ROWS_SENDS)

    def exchange_inner(index):
        for pair in range(1, 5):
            unpack(index, pair, 1)
        for copy in copies[index][n_rows_sends:]:
            copy.wait_recv()
        for pair in range(1, 5):
            unpack(index, pair, 0)
            unpack(index, pair, 2)

    def exchange_outer(index):
        for copy in copies[index][:n_rows_sends]:
            copy.wait_recv()
        for block in range(3):
            unpack(index, 0, block)
            unpack(index, 5, block)

    loads[0].wait()
    state[...] = jnp.swapaxes(x_in[...].reshape(TL, ROWS, COLS), 0, 1)
    for pair in range(4):
        put_tiles(0, pair, state[2 * pair], state[2 * pair + 1])
    for load in loads[1:4]:
        load.wait()
    build_conv_in(w1_raw, embed_raw, w1_turned, w1)
    build_conv_out(w2_raw, w2)
    pl.semaphore_wait(barrier, len(NEIGHBOURS))
    for copy in copies[0]:
        copy.start()
    for load in loads[4:]:
        load.wait()
    build_guide(count, obs_step, obs_row, obs_col, obs_value, guide)
    turned_first[...] = jnp.swapaxes(first[...].reshape(TL, ROWS, COLS), 0, 1)
    turned_second[...] = jnp.swapaxes(second[...].reshape(TL, ROWS, COLS), 0, 1)

    exchange_inner(0)
    for at in range(0, len(INNER_BANDS), 6):
        hidden_bands(0, INNER_BANDS[at : at + 6])
    for pair in (1, 2):
        step_pair(pair)
    for copy in copies[1][n_rows_sends + 2 :]:
        copy.start()
    exchange_outer(0)
    for at in range(0, len(OUTER_BANDS), 6):
        hidden_bands(0, OUTER_BANDS[at : at + 6])
    for pair in (0, 3):
        step_pair(pair)
    for copy in copies[1][: n_rows_sends + 2]:
        copy.start()

    exchange_inner(1)
    for at in range(0, len(INNER_BANDS), 6):
        hidden_bands(1, INNER_BANDS[at : at + 6])
    exchange_outer(1)
    for at in range(0, len(OUTER_BANDS), 6):
        hidden_bands(1, OUTER_BANDS[at : at + 6])
    done = jnp.stack([finish_row(1, r, turned_second) for r in range(ROWS)], axis=0)
    out[...] = jnp.swapaxes(done, 0, 1).reshape(TL * ROWS, COLS)
    for index in range(2):
        for copy in copies[index]:
            copy.wait_send()


def per_device(
    sizes,
    noisy_states,
    noise_first,
    noise_second,
    conv_in,
    conv_out,
    level_embed,
    obs_count,
    obs_step,
    obs_row,
    obs_col,
    obs_value,
):
    flat = (TL * ROWS, COLS)
    slots = (1, SLOTS)
    far = pl.BlockSpec(memory_space=pltpu.HBM)
    result = pl.pallas_call(
        functools.partial(kernel, sizes),
        out_shape=pltpu.VMEM(flat, jnp.float32),
        in_specs=[far] * 6 + [pl.BlockSpec(memory_space=pltpu.SMEM)] + [far] * 4,
        out_specs=pl.BlockSpec(memory_space=pltpu.VMEM),
        scratch_shapes=[
            pltpu.VMEM(flat, jnp.float32),
            pltpu.VMEM(flat, jnp.float32),
            pltpu.VMEM(flat, jnp.float32),
            pltpu.VMEM((9, C_IN, HID), jnp.bfloat16),
            pltpu.VMEM((9, LAYERS, HID), jnp.bfloat16),
            pltpu.VMEM((1, HID), jnp.float32),
            pltpu.VMEM(slots, jnp.int32),
            pltpu.VMEM(slots, jnp.int32),
            pltpu.VMEM(slots, jnp.int32),
            pltpu.VMEM(slots, jnp.float32),
            pltpu.VMEM((ROWS, TL, COLS), jnp.float32),
            pltpu.VMEM((ROWS, TL, COLS), jnp.float32),
            pltpu.VMEM((ROWS, TL, COLS), jnp.float32),
            pltpu.VMEM((256, 128), jnp.float32),
            pltpu.VMEM((T * HID, K_IN), jnp.bfloat16),
            pltpu.VMEM((72, T * HID), jnp.bfloat16),
            pltpu.VMEM((2 * ROWS * TL, COLS), jnp.float32),
            pltpu.VMEM((2, 3, PAIRS, 16, COLS), jnp.bfloat16),
            pltpu.VMEM((2 * PAIRS * 72, COLS), jnp.float32),
            pltpu.VMEM((BANDS, 72, COLS), jnp.float32),
            pltpu.SemaphoreType.DMA((10,)),
            pltpu.SemaphoreType.DMA((2, len(SENDS))),
            pltpu.SemaphoreType.DMA((2, len(SENDS))),
        ],
        compiler_params=pltpu.CompilerParams(
            collective_id=0, has_side_effects=True, vmem_limit_bytes=32 * 1024 * 1024
        ),
        name="reverse_steps",
    )(
        *(
            operand if operand is obs_count else pltpu.with_memory_space_constraint(operand, pltpu.HBM)
            for operand in (
                noisy_states.reshape(flat),
                noise_first.reshape(flat),
                noise_second.reshape(flat),
                jnp.swapaxes(conv_in, 1, 2),
                conv_out,
                level_embed.reshape(1, HID),
                obs_count,
                obs_step.reshape(slots),
                obs_row.reshape(slots),
                obs_col.reshape(slots),
                obs_value.reshape(slots),
            )
        )
    )
    return result.reshape(noisy_states.shape)


def solution(mesh):
    sizes = (mesh.shape["tm"], mesh.shape["rows"])
    cells = P("tm", None, "rows", None)
    block = P("tm", "rows", None)
    return jax.shard_map(
        functools.partial(per_device, sizes),
        mesh=mesh,
        in_specs=(cells, cells, cells, P(), P(), P(), P("tm", "rows"), block, block, block, block),
        out_specs=cells,
        check_vma=False,
    )
```

```python
import functools

import jax
import jax.numpy as jnp
from jax import lax
from jax.experimental import pallas as pl
from jax.experimental.pallas import tpu as pltpu
from jax.sharding import PartitionSpec as P

MESH = pl.DeviceIdType.MESH
LEVELS = (1.0, 0.5, 0.2)
OBS_NOISE = 0.1
COVARIANCE_GAIN = 0.5
T = 4
LAYERS = 2
TL = 8
ROWS = 8
COLS = 256
HID = 96
C_IN = 18
SLOTS = 256
PAIRS = 6
BANDS = 10
K_IN = 224
NEIGHBOURS = ((0, -1), (0, 1), (-1, -1), (1, -1), (-1, 1), (1, 1), (-1, 0), (1, 0))
SLOT_OF = (0, 1, 4, 5, 2, 3)
FAR, NEAR, EDGES, MIDS = slice(0, 3), slice(3, 6), slice(6, 8), slice(8, 10)
INNER_BANDS = (4, 5, 2, 3, 6, 7)


def three_parts(values):
    high = values.astype(jnp.bfloat16).astype(jnp.float32)
    rest = values - high
    mid = rest.astype(jnp.bfloat16).astype(jnp.float32)
    return high, mid, rest - mid


def build_conv_in(w1_raw, embed_raw, w1_turned, w1):
    w1_turned[...] = jnp.zeros(w1_turned.shape, jnp.float32)
    for off in range(9):
        w1_turned[24 * off : 24 * off + C_IN, 0:HID] = w1_raw[off].astype(jnp.float32) * 0.5
    parts = three_parts(embed_raw[...] * 0.5)
    for piece in range(3):
        w1_turned[216 + piece : 217 + piece, 0:HID] = parts[piece]
    base = jnp.transpose(w1_turned[...])[:HID]
    lane = lax.broadcasted_iota(jnp.int32, (HID, 256), 1)
    for t in range(T):
        shifted = jnp.where(lane < 216, pltpu.roll(base, 2 * t, 1), base) if t else base
        w1[t * HID : (t + 1) * HID, :] = shifted[:, :K_IN].astype(jnp.bfloat16)


def build_conv_out(w2_raw, w2):
    sub = lax.broadcasted_iota(jnp.int32, (TL, HID), 0)
    pieces = []
    for b in range(3):
        for a in range(3):
            taps = w2_raw[3 * a + b].astype(jnp.float32)
            pieces.append(
                jnp.where(
                    sub % 2 == 0,
                    jnp.broadcast_to(taps[0:1], (TL, HID)),
                    jnp.broadcast_to(taps[1:2], (TL, HID)),
                )
            )
    tall = jnp.concatenate(pieces, axis=0)
    wide = jnp.concatenate([tall, jnp.zeros((72, T * HID - HID), jnp.float32)], axis=1)
    state = (lax.broadcasted_iota(jnp.int32, (72, T * HID), 0) % TL) // 2
    total = jnp.where(state == 0, wide, 0.0)
    for t in range(1, T):
        total = total + jnp.where(state == t, pltpu.roll(wide, t * HID, 1), 0.0)
    w2[...] = total.astype(jnp.bfloat16)


def build_guide(count, obs_step, obs_row, obs_col, obs_value, guide):
    slot = lax.broadcasted_iota(jnp.int32, (1, SLOTS), 1)
    live = slot < count[0, 0]
    cell = jnp.where(live, obs_row[...] * TL + obs_step[...] * LAYERS, -1)
    hot = lax.broadcasted_iota(jnp.int32, (ROWS * TL, SLOTS), 0) == cell
    high, mid, low = three_parts(obs_value[...])
    left = jnp.concatenate(
        [
            jnp.where(hot, 1.0, 0.0),
            jnp.where(hot, high, 0.0),
            jnp.where(hot, mid, 0.0),
            jnp.where(hot, low, 0.0),
        ],
        axis=0,
    ).astype(jnp.bfloat16)
    right = jnp.where(
        lax.broadcasted_iota(jnp.int32, (COLS, SLOTS), 0) == obs_col[...], 1.0, 0.0
    ).astype(jnp.bfloat16)
    found = lax.dot_general(left, right, (((1,), (1,)), ((), ())), preferred_element_type=jnp.float32)
    rows = ROWS * TL
    guide[0:rows, :] = found[0:rows]
    guide[rows : 2 * rows, :] = (
        found[rows : 2 * rows] + found[2 * rows : 3 * rows] + found[3 * rows : 4 * rows]
    )


def kernel(
    sizes,
    x_hbm,
    first_hbm,
    second_hbm,
    w1_hbm,
    w2_hbm,
    embed_hbm,
    count,
    step_hbm,
    row_hbm,
    col_hbm,
    value_hbm,
    out,
    x_in,
    first,
    second,
    w1_raw,
    w2_raw,
    embed_raw,
    obs_step,
    obs_row,
    obs_col,
    obs_value,
    state,
    shift,
    slope,
    w1_turned,
    w1,
    w2,
    guide,
    tiles,
    frames,
    taps,
    load_sems,
    send_sems,
    recv_sems,
):
    n_tm, n_rows = sizes
    tm = lax.axis_index("tm")
    rw = lax.axis_index("rows")

    def peer(dt, dr):
        return {
            "tm": lax.rem(tm + dt + n_tm, n_tm) if dt else tm,
            "rows": lax.rem(rw + dr + n_rows, n_rows) if dr else rw,
        }

    barrier = pltpu.get_barrier_semaphore()
    for dt, dr in NEIGHBOURS:
        pl.semaphore_signal(barrier, inc=1, device_id=peer(dt, dr), device_id_type=MESH)

    loads = [
        pltpu.make_async_copy(src, dst, load_sems.at[i])
        for i, (src, dst) in enumerate(
            (
                (x_hbm, x_in),
                (w1_hbm, w1_raw),
                (embed_hbm, embed_raw),
                (w2_hbm, w2_raw),
                (step_hbm, obs_step),
                (row_hbm, obs_row),
                (col_hbm, obs_col),
                (value_hbm, obs_value),
                (first_hbm, first),
                (second_hbm, second),
            )
        )
    ]
    for load in loads:
        load.start()

    far_side = lax.rem(rw, 2)
    near_side = 1 - far_side

    def copy_to(index, k, dt, rows_to, source, target):
        return pltpu.make_async_remote_copy(
            src_ref=tiles.at[index, 1, source],
            dst_ref=tiles.at[index, 1 - dt, target],
            send_sem=send_sems.at[index, k],
            recv_sem=recv_sems.at[index, k],
            device_id={"tm": peer(dt, 0)["tm"], "rows": rows_to},
            device_id_type=MESH,
        )

    copies = []
    for index in range(2):
        made = []
        for side in (far_side, near_side):
            rows_to = lax.rem(rw + 2 * side - 1 + n_rows, n_rows)
            for dt in (-1, 1, 0):
                made.append(
                    copy_to(index, len(made), dt, rows_to, pl.ds(1 + side, 1), pl.ds(3 - 3 * side, 1))
                )
        for part in (slice(1, 3), slice(4, 6)):
            for dt in (-1, 1):
                made.append(copy_to(index, len(made), dt, rw, part, part))
        copies.append(made)

    def put_tiles(index, slot, upper, lower):
        scale = 1.0 / (1.0 + LEVELS[index] ** 2) ** 0.5
        tile = jnp.concatenate([upper, lower], axis=0) * scale
        tiles[index, 1, slot] = tile.astype(jnp.bfloat16)

    def unpack(index, slot, at_row, block):
        tile = tiles[index, block, slot].astype(jnp.float32)
        if block == 0:
            tile = jnp.where(tm == 0, 0.0, tile)
        if block == 2:
            tile = jnp.where(tm == n_tm - 1, 0.0, tile)
        for b in range(3):
            moved = pltpu.roll(tile, (1 - b) % COLS, 1) if b != 1 else tile
            for half in range(2):
                at = pl.multiple_of((at_row + half) * 72 + b * 24 + block * 8, 8)
                frames[pl.ds(at, 8), :] = moved[half * 8 : half * 8 + 8]

    def hidden_bands(index, group):
        ones = jnp.full((K_IN - 216, COLS), LEVELS[index], jnp.float32)
        windows = jnp.concatenate(
            [
                jnp.concatenate([frames[pl.ds(pl.multiple_of(72 * j, 8), 216), :], ones], axis=0).astype(
                    jnp.bfloat16
                )
                for j in group
            ],
            axis=1,
        )
        half = jnp.dot(w1[...], windows, preferred_element_type=jnp.float32)
        hidden = (half + half * jnp.tanh(half)).astype(jnp.bfloat16)
        found = jnp.dot(w2[...], hidden, preferred_element_type=jnp.float32)
        for k, j in enumerate(group):
            taps[j] = found[:, k * COLS : (k + 1) * COLS]

    def prepare_rows(index, noise):
        level_now, level_next = LEVELS[index], LEVELS[index + 1]
        base = 1.0 + level_now**2
        spread = level_now**2 - level_next**2
        keep = 1.0 / level_now**2
        gain = 1.0 / (OBS_NOISE + COVARIANCE_GAIN * level_now**2)
        turned = jnp.swapaxes(noise[...].reshape(TL, ROWS, COLS), 0, 1)
        for r in range(ROWS):
            current = state[r]
            hits = guide[r * 8 : r * 8 + 8, :]
            values = guide[64 + r * 8 : 64 + r * 8 + 8, :]
            still = current * (1.0 / base)
            score = (still - current) * keep + (values - hits * still) * gain
            shift[r] = current + spread * score + spread**0.5 * turned[r]
            slope[r] = (spread * level_now / base**0.5) * (keep - gain * hits)

    def finish_row(r):
        sums = [
            taps[r, b * 24 : b * 24 + 8, :]
            + taps[r + 1, b * 24 + 8 : b * 24 + 16, :]
            + taps[r + 2, b * 24 + 16 : b * 24 + 24, :]
            for b in range(3)
        ]
        net = sums[1] + pltpu.roll(sums[0], 1, 1) + pltpu.roll(sums[2], COLS - 1, 1)
        slab = shift[r] + slope[r] * net
        state[r] = slab
        return slab

    def finish_pair(index, pair, slot):
        slabs = [finish_row(2 * pair + half) for half in range(2)]
        if index == 0:
            put_tiles(1, slot, *slabs)

    def exchange_inner(index):
        for pair in range(1, 5):
            unpack(index, SLOT_OF[pair], 2 * pair, 1)
        for part in (EDGES, MIDS):
            for copy in copies[index][part]:
                copy.wait_recv()
        for pair in range(1, 5):
            unpack(index, SLOT_OF[pair], 2 * pair, 0)
            unpack(index, SLOT_OF[pair], 2 * pair, 2)
        hidden_bands(index, INNER_BANDS)
        for pair in (1, 2):
            finish_pair(index, pair, SLOT_OF[pair + 1])

    def exchange_outer(index, side, part):
        for copy in copies[index][part]:
            copy.wait_recv()
        for block in range(3):
            unpack(index, 3 * side, 10 * side, block)
        hidden_bands(index, (8 * side, 8 * side + 1))
        finish_pair(index, 3 * side, 1 + side)

    def start(index, part):
        for copy in copies[index][part]:
            copy.start()

    loads[0].wait()
    state[...] = jnp.swapaxes(x_in[...].reshape(TL, ROWS, COLS), 0, 1)
    for pair in range(4):
        put_tiles(0, SLOT_OF[pair + 1], state[2 * pair], state[2 * pair + 1])
    for load in loads[1:4]:
        load.wait()
    build_conv_in(w1_raw, embed_raw, w1_turned, w1)
    build_conv_out(w2_raw, w2)
    pl.semaphore_wait(barrier, len(NEIGHBOURS))
    for part in (FAR, NEAR, EDGES, MIDS):
        start(0, part)
    for load in loads[4:]:
        load.wait()
    build_guide(count, obs_step, obs_row, obs_col, obs_value, guide)
    prepare_rows(0, first)

    exchange_inner(0)
    start(1, MIDS)
    exchange_outer(0, near_side, NEAR)
    start(1, NEAR)
    exchange_outer(0, far_side, FAR)
    start(1, FAR)
    start(1, EDGES)
    prepare_rows(1, second)
    exchange_inner(1)
    exchange_outer(1, near_side, NEAR)
    exchange_outer(1, far_side, FAR)
    out[...] = jnp.swapaxes(state[...], 0, 1).reshape(TL * ROWS, COLS)
    for index in range(2):
        for copy in copies[index]:
            copy.wait_send()


def per_device(
    sizes,
    noisy_states,
    noise_first,
    noise_second,
    conv_in,
    conv_out,
    level_embed,
    obs_count,
    obs_step,
    obs_row,
    obs_col,
    obs_value,
):
    flat = (TL * ROWS, COLS)
    slots = (1, SLOTS)
    far = pl.BlockSpec(memory_space=pltpu.HBM)
    result = pl.pallas_call(
        functools.partial(kernel, sizes),
        out_shape=pltpu.VMEM(flat, jnp.float32),
        in_specs=[far] * 6 + [pl.BlockSpec(memory_space=pltpu.SMEM)] + [far] * 4,
        out_specs=pl.BlockSpec(memory_space=pltpu.VMEM),
        scratch_shapes=[
            pltpu.VMEM(flat, jnp.float32),
            pltpu.VMEM(flat, jnp.float32),
            pltpu.VMEM(flat, jnp.float32),
            pltpu.VMEM((9, C_IN, HID), jnp.bfloat16),
            pltpu.VMEM((9, LAYERS, HID), jnp.bfloat16),
            pltpu.VMEM((1, HID), jnp.float32),
            pltpu.VMEM(slots, jnp.int32),
            pltpu.VMEM(slots, jnp.int32),
            pltpu.VMEM(slots, jnp.int32),
            pltpu.VMEM(slots, jnp.float32),
            pltpu.VMEM((ROWS, TL, COLS), jnp.float32),
            pltpu.VMEM((ROWS, TL, COLS), jnp.float32),
            pltpu.VMEM((ROWS, TL, COLS), jnp.float32),
            pltpu.VMEM((256, 128), jnp.float32),
            pltpu.VMEM((T * HID, K_IN), jnp.bfloat16),
            pltpu.VMEM((72, T * HID), jnp.bfloat16),
            pltpu.VMEM((2 * ROWS * TL, COLS), jnp.float32),
            pltpu.VMEM((2, 3, PAIRS, 16, COLS), jnp.bfloat16),
            pltpu.VMEM((2 * PAIRS * 72, COLS), jnp.float32),
            pltpu.VMEM((BANDS, 72, COLS), jnp.float32),
            pltpu.SemaphoreType.DMA((10,)),
            pltpu.SemaphoreType.DMA((2, 10)),
            pltpu.SemaphoreType.DMA((2, 10)),
        ],
        compiler_params=pltpu.CompilerParams(
            collective_id=0, has_side_effects=True, vmem_limit_bytes=32 * 1024 * 1024
        ),
        name="reverse_steps",
    )(
        *(
            operand if operand is obs_count else pltpu.with_memory_space_constraint(operand, pltpu.HBM)
            for operand in (
                noisy_states.reshape(flat),
                noise_first.reshape(flat),
                noise_second.reshape(flat),
                jnp.swapaxes(conv_in, 1, 2),
                conv_out,
                level_embed.reshape(1, HID),
                obs_count,
                obs_step.reshape(slots),
                obs_row.reshape(slots),
                obs_col.reshape(slots),
                obs_value.reshape(slots),
            )
        )
    )
    return result.reshape(noisy_states.shape)


def solution(mesh):
    sizes = (mesh.shape["tm"], mesh.shape["rows"])
    cells = P("tm", None, "rows", None)
    block = P("tm", "rows", None)
    return jax.shard_map(
        functools.partial(per_device, sizes),
        mesh=mesh,
        in_specs=(cells, cells, cells, P(), P(), P(), P("tm", "rows"), block, block, block, block),
        out_specs=cells,
        check_vma=False,
    )
```

```python
import functools

import jax
import jax.numpy as jnp
from jax import lax
from jax.experimental import pallas as pl
from jax.experimental.pallas import tpu as pltpu
from jax.sharding import PartitionSpec as P

MESH = pl.DeviceIdType.MESH
LEVELS = (1.0, 0.5, 0.2)
OBS_NOISE = 0.1
COVARIANCE_GAIN = 0.5
T = 4
LAYERS = 2
TL = 8
ROWS = 8
COLS = 256
HID = 96
C_IN = 18
SLOTS = 256
PAIRS = 6
BANDS = 10
K_IN = 224
NEIGHBOURS = ((0, -1), (0, 1), (-1, -1), (1, -1), (-1, 1), (1, 1), (-1, 0), (1, 0))
SLOT_OF = (0, 1, 4, 5, 2, 3)
FAR, NEAR, EDGES, MIDS = slice(0, 3), slice(3, 6), slice(6, 8), slice(8, 10)
INNER_BANDS = (4, 5, 2, 3, 6, 7)


def three_parts(values):
    high = values.astype(jnp.bfloat16).astype(jnp.float32)
    rest = values - high
    mid = rest.astype(jnp.bfloat16).astype(jnp.float32)
    return high, mid, rest - mid


def build_conv_in(w1_raw, embed_raw, w1_turned, w1):
    w1_turned[...] = jnp.zeros(w1_turned.shape, jnp.float32)
    for off in range(9):
        w1_turned[24 * off : 24 * off + C_IN, 0:HID] = w1_raw[off].astype(jnp.float32) * 0.5
    parts = three_parts(embed_raw[...] * 0.5)
    for piece in range(3):
        w1_turned[216 + piece : 217 + piece, 0:HID] = parts[piece]
    base = jnp.transpose(w1_turned[...])[:HID]
    lane = lax.broadcasted_iota(jnp.int32, (HID, 256), 1)
    for t in range(T):
        shifted = jnp.where(lane < 216, pltpu.roll(base, 2 * t, 1), base) if t else base
        w1[t * HID : (t + 1) * HID, :] = shifted[:, :K_IN].astype(jnp.bfloat16)


def build_conv_out(w2_raw, w2):
    sub = lax.broadcasted_iota(jnp.int32, (TL, HID), 0)
    pieces = []
    for b in range(3):
        for a in range(3):
            taps = w2_raw[3 * a + b].astype(jnp.float32)
            pieces.append(
                jnp.where(
                    sub % 2 == 0,
                    jnp.broadcast_to(taps[0:1], (TL, HID)),
                    jnp.broadcast_to(taps[1:2], (TL, HID)),
                )
            )
    tall = jnp.concatenate(pieces, axis=0)
    wide = jnp.concatenate([tall, jnp.zeros((72, T * HID - HID), jnp.float32)], axis=1)
    state = (lax.broadcasted_iota(jnp.int32, (72, T * HID), 0) % TL) // 2
    total = jnp.where(state == 0, wide, 0.0)
    for t in range(1, T):
        total = total + jnp.where(state == t, pltpu.roll(wide, t * HID, 1), 0.0)
    w2[...] = total.astype(jnp.bfloat16)


def build_guide(count, obs_step, obs_row, obs_col, obs_value, guide):
    slot = lax.broadcasted_iota(jnp.int32, (1, SLOTS), 1)
    live = slot < count[0, 0]
    cell = jnp.where(live, obs_row[...] * TL + obs_step[...] * LAYERS, -1)
    hot = lax.broadcasted_iota(jnp.int32, (ROWS * TL, SLOTS), 0) == cell
    high, mid, low = three_parts(obs_value[...])
    left = jnp.concatenate(
        [
            jnp.where(hot, 1.0, 0.0),
            jnp.where(hot, high, 0.0),
            jnp.where(hot, mid, 0.0),
            jnp.where(hot, low, 0.0),
        ],
        axis=0,
    ).astype(jnp.bfloat16)
    right = jnp.where(
        lax.broadcasted_iota(jnp.int32, (COLS, SLOTS), 0) == obs_col[...], 1.0, 0.0
    ).astype(jnp.bfloat16)
    found = lax.dot_general(left, right, (((1,), (1,)), ((), ())), preferred_element_type=jnp.float32)
    rows = ROWS * TL
    guide[0:rows, :] = found[0:rows]
    guide[rows : 2 * rows, :] = (
        found[rows : 2 * rows] + found[2 * rows : 3 * rows] + found[3 * rows : 4 * rows]
    )


def kernel(
    sizes,
    x_hbm,
    first_hbm,
    second_hbm,
    w1_hbm,
    w2_hbm,
    embed_hbm,
    count,
    step_hbm,
    row_hbm,
    col_hbm,
    value_hbm,
    out,
    x_in,
    first,
    second,
    w1_raw,
    w2_raw,
    embed_raw,
    obs_step,
    obs_row,
    obs_col,
    obs_value,
    state,
    shift,
    slope,
    w1_turned,
    w1,
    w2,
    guide,
    tiles,
    frames,
    taps,
    load_sems,
    send_sems,
    recv_sems,
):
    n_tm, n_rows = sizes
    tm = lax.axis_index("tm")
    rw = lax.axis_index("rows")

    def peer(dt, dr):
        return {
            "tm": lax.rem(tm + dt + n_tm, n_tm) if dt else tm,
            "rows": lax.rem(rw + dr + n_rows, n_rows) if dr else rw,
        }

    barrier = pltpu.get_barrier_semaphore()
    for dt, dr in NEIGHBOURS:
        pl.semaphore_signal(barrier, inc=1, device_id=peer(dt, dr), device_id_type=MESH)

    loads = [
        pltpu.make_async_copy(src, dst, load_sems.at[i])
        for i, (src, dst) in enumerate(
            (
                (x_hbm, x_in),
                (w1_hbm, w1_raw),
                (embed_hbm, embed_raw),
                (w2_hbm, w2_raw),
                (step_hbm, obs_step),
                (row_hbm, obs_row),
                (col_hbm, obs_col),
                (value_hbm, obs_value),
                (first_hbm, first),
                (second_hbm, second),
            )
        )
    ]
    for load in loads:
        load.start()

    far_side = lax.rem(rw, 2)
    near_side = 1 - far_side

    def copy_to(index, k, dt, rows_to, source, target):
        return pltpu.make_async_remote_copy(
            src_ref=tiles.at[index, 1, source],
            dst_ref=tiles.at[index, 1 - dt, target],
            send_sem=send_sems.at[index, k],
            recv_sem=recv_sems.at[index, k],
            device_id={"tm": peer(dt, 0)["tm"], "rows": rows_to},
            device_id_type=MESH,
        )

    copies = []
    for index in range(2):
        made = []
        for side in (far_side, near_side):
            rows_to = lax.rem(rw + 2 * side - 1 + n_rows, n_rows)
            for dt in (-1, 1, 0):
                made.append(
                    copy_to(index, len(made), dt, rows_to, pl.ds(1 + side, 1), pl.ds(3 - 3 * side, 1))
                )
        for part in (slice(1, 3), slice(4, 6)):
            for dt in (-1, 1):
                made.append(copy_to(index, len(made), dt, rw, part, part))
        copies.append(made)

    def put_tiles(index, slot, upper, lower):
        scale = 1.0 / (1.0 + LEVELS[index] ** 2) ** 0.5
        tile = jnp.concatenate([upper, lower], axis=0) * scale
        tiles[index, 1, slot] = tile.astype(jnp.bfloat16)

    def unpack(index, slot, at_row, block):
        tile = tiles[index, block, slot].astype(jnp.float32)
        if block == 0:
            tile = jnp.where(tm == 0, 0.0, tile)
        if block == 2:
            tile = jnp.where(tm == n_tm - 1, 0.0, tile)
        for b in range(3):
            moved = pltpu.roll(tile, (1 - b) % COLS, 1) if b != 1 else tile
            for half in range(2):
                at = pl.multiple_of((at_row + half) * 72 + b * 24 + block * 8, 8)
                frames[pl.ds(at, 8), :] = moved[half * 8 : half * 8 + 8]

    def hidden_bands(index, group):
        ones = jnp.full((K_IN - 216, COLS), LEVELS[index], jnp.float32)
        windows = jnp.concatenate(
            [
                jnp.concatenate([frames[pl.ds(pl.multiple_of(72 * j, 8), 216), :], ones], axis=0).astype(
                    jnp.bfloat16
                )
                for j in group
            ],
            axis=1,
        )
        half = jnp.dot(w1[...], windows, preferred_element_type=jnp.float32)
        hidden = (half + half * jnp.tanh(half)).astype(jnp.bfloat16)
        found = jnp.dot(w2[...], hidden, preferred_element_type=jnp.float32)
        for k, j in enumerate(group):
            taps[j] = found[:, k * COLS : (k + 1) * COLS]

    def prepare_rows(index, noise):
        level_now, level_next = LEVELS[index], LEVELS[index + 1]
        base = 1.0 + level_now**2
        spread = level_now**2 - level_next**2
        keep = 1.0 / level_now**2
        gain = 1.0 / (OBS_NOISE + COVARIANCE_GAIN * level_now**2)
        turned = jnp.swapaxes(noise[...].reshape(TL, ROWS, COLS), 0, 1)
        for r in range(ROWS):
            current = state[r]
            hits = guide[r * 8 : r * 8 + 8, :]
            values = guide[64 + r * 8 : 64 + r * 8 + 8, :]
            still = current * (1.0 / base)
            score = (still - current) * keep + (values - hits * still) * gain
            shift[r] = current + spread * score + spread**0.5 * turned[r]
            slope[r] = (spread * level_now / base**0.5) * (keep - gain * hits)

    def finish_row(r):
        sums = [
            taps[r, b * 24 : b * 24 + 8, :]
            + taps[r + 1, b * 24 + 8 : b * 24 + 16, :]
            + taps[r + 2, b * 24 + 16 : b * 24 + 24, :]
            for b in range(3)
        ]
        net = sums[1] + pltpu.roll(sums[0], 1, 1) + pltpu.roll(sums[2], COLS - 1, 1)
        slab = shift[r] + slope[r] * net
        state[r] = slab
        return slab

    def finish_pair(index, pair, slot):
        slabs = [finish_row(2 * pair + half) for half in range(2)]
        if index == 0:
            put_tiles(1, slot, *slabs)

    def exchange_inner(index):
        for pair in range(1, 5):
            unpack(index, SLOT_OF[pair], 2 * pair, 1)
        for part in (EDGES, MIDS):
            for copy in copies[index][part]:
                copy.wait_recv()
        for pair in range(1, 5):
            unpack(index, SLOT_OF[pair], 2 * pair, 0)
            unpack(index, SLOT_OF[pair], 2 * pair, 2)
        hidden_bands(index, INNER_BANDS)
        for pair in (1, 2):
            finish_pair(index, pair, SLOT_OF[pair + 1])

    def exchange_outer(index, side, part):
        for copy in copies[index][part]:
            copy.wait_recv()
        for block in range(3):
            unpack(index, 3 * side, 10 * side, block)
        hidden_bands(index, (8 * side, 8 * side + 1))
        finish_pair(index, 3 * side, 1 + side)

    def start(index, part):
        for copy in copies[index][part]:
            copy.start()

    loads[0].wait()
    state[...] = jnp.swapaxes(x_in[...].reshape(TL, ROWS, COLS), 0, 1)
    for pair in range(4):
        put_tiles(0, SLOT_OF[pair + 1], state[2 * pair], state[2 * pair + 1])
    pl.semaphore_wait(barrier, len(NEIGHBOURS))
    start(0, FAR)
    for load in loads[1:]:
        load.wait()
    start(0, NEAR)
    build_conv_in(w1_raw, embed_raw, w1_turned, w1)
    start(0, EDGES)
    start(0, MIDS)
    build_conv_out(w2_raw, w2)
    build_guide(count, obs_step, obs_row, obs_col, obs_value, guide)
    prepare_rows(0, first)

    exchange_inner(0)
    start(1, MIDS)
    exchange_outer(0, near_side, NEAR)
    start(1, NEAR)
    exchange_outer(0, far_side, FAR)
    start(1, FAR)
    start(1, EDGES)
    prepare_rows(1, second)
    exchange_inner(1)
    exchange_outer(1, near_side, NEAR)
    for index in range(2):
        for copy in copies[index]:
            copy.wait_send()
    exchange_outer(1, far_side, FAR)
    out[...] = jnp.swapaxes(state[...], 0, 1).reshape(TL * ROWS, COLS)


def per_device(
    sizes,
    noisy_states,
    noise_first,
    noise_second,
    conv_in,
    conv_out,
    level_embed,
    obs_count,
    obs_step,
    obs_row,
    obs_col,
    obs_value,
):
    flat = (TL * ROWS, COLS)
    slots = (1, SLOTS)
    far = pl.BlockSpec(memory_space=pltpu.HBM)
    result = pl.pallas_call(
        functools.partial(kernel, sizes),
        out_shape=pltpu.VMEM(flat, jnp.float32),
        in_specs=[far] * 6 + [pl.BlockSpec(memory_space=pltpu.SMEM)] + [far] * 4,
        out_specs=pl.BlockSpec(memory_space=pltpu.VMEM),
        scratch_shapes=[
            pltpu.VMEM(flat, jnp.float32),
            pltpu.VMEM(flat, jnp.float32),
            pltpu.VMEM(flat, jnp.float32),
            pltpu.VMEM((9, C_IN, HID), jnp.bfloat16),
            pltpu.VMEM((9, LAYERS, HID), jnp.bfloat16),
            pltpu.VMEM((1, HID), jnp.float32),
            pltpu.VMEM(slots, jnp.int32),
            pltpu.VMEM(slots, jnp.int32),
            pltpu.VMEM(slots, jnp.int32),
            pltpu.VMEM(slots, jnp.float32),
            pltpu.VMEM((ROWS, TL, COLS), jnp.float32),
            pltpu.VMEM((ROWS, TL, COLS), jnp.float32),
            pltpu.VMEM((ROWS, TL, COLS), jnp.float32),
            pltpu.VMEM((256, 128), jnp.float32),
            pltpu.VMEM((T * HID, K_IN), jnp.bfloat16),
            pltpu.VMEM((72, T * HID), jnp.bfloat16),
            pltpu.VMEM((2 * ROWS * TL, COLS), jnp.float32),
            pltpu.VMEM((2, 3, PAIRS, 16, COLS), jnp.bfloat16),
            pltpu.VMEM((2 * PAIRS * 72, COLS), jnp.float32),
            pltpu.VMEM((BANDS, 72, COLS), jnp.float32),
            pltpu.SemaphoreType.DMA((10,)),
            pltpu.SemaphoreType.DMA((2, 10)),
            pltpu.SemaphoreType.DMA((2, 10)),
        ],
        compiler_params=pltpu.CompilerParams(
            collective_id=0, has_side_effects=True, vmem_limit_bytes=32 * 1024 * 1024
        ),
        name="reverse_steps",
    )(
        *(
            operand if operand is obs_count else pltpu.with_memory_space_constraint(operand, pltpu.HBM)
            for operand in (
                noisy_states.reshape(flat),
                noise_first.reshape(flat),
                noise_second.reshape(flat),
                jnp.swapaxes(conv_in, 1, 2),
                conv_out,
                level_embed.reshape(1, HID),
                obs_count,
                obs_step.reshape(slots),
                obs_row.reshape(slots),
                obs_col.reshape(slots),
                obs_value.reshape(slots),
            )
        )
    )
    return result.reshape(noisy_states.shape)


def solution(mesh):
    sizes = (mesh.shape["tm"], mesh.shape["rows"])
    cells = P("tm", None, "rows", None)
    block = P("tm", "rows", None)
    return jax.shard_map(
        functools.partial(per_device, sizes),
        mesh=mesh,
        in_specs=(cells, cells, cells, P(), P(), P(), P("tm", "rows"), block, block, block, block),
        out_specs=cells,
        check_vma=False,
    )
```

```python
import functools

import jax
import jax.numpy as jnp
from jax import lax
from jax.experimental import pallas as pl
from jax.experimental.pallas import tpu as pltpu
from jax.sharding import PartitionSpec as P

MESH = pl.DeviceIdType.MESH
LEVELS = (1.0, 0.5, 0.2)
OBS_NOISE = 0.1
COVARIANCE_GAIN = 0.5
T = 4
LAYERS = 2
TL = 8
ROWS = 8
COLS = 256
HID = 96
C_IN = 18
SLOTS = 256
PAIRS = 6
BANDS = 10
K_IN = 224
NEIGHBOURS = ((0, -1), (0, 1), (-1, -1), (1, -1), (-1, 1), (1, 1), (-1, 0), (1, 0))
SLOT_OF = (0, 1, 4, 5, 2, 3)
FAR, NEAR, EDGES, MIDS = slice(0, 3), slice(3, 6), slice(6, 8), slice(8, 10)
INNER_BANDS = (4, 5, 2, 3, 6, 7)


def three_parts(values):
    high = values.astype(jnp.bfloat16).astype(jnp.float32)
    rest = values - high
    mid = rest.astype(jnp.bfloat16).astype(jnp.float32)
    return high, mid, rest - mid


def build_conv_in(w1_raw, embed_raw, w1_turned, w1):
    w1_turned[...] = jnp.zeros(w1_turned.shape, jnp.float32)
    for off in range(9):
        w1_turned[24 * off : 24 * off + C_IN, 0:HID] = w1_raw[off].astype(jnp.float32) * 0.5
    parts = three_parts(embed_raw[...] * 0.5)
    for piece in range(3):
        w1_turned[216 + piece : 217 + piece, 0:HID] = parts[piece]
    base = jnp.transpose(w1_turned[...])[:HID]
    lane = lax.broadcasted_iota(jnp.int32, (HID, 256), 1)
    for t in range(T):
        shifted = jnp.where(lane < 216, pltpu.roll(base, 2 * t, 1), base) if t else base
        w1[t * HID : (t + 1) * HID, :] = shifted[:, :K_IN].astype(jnp.bfloat16)


def build_conv_out(w2_raw, w2):
    sub = lax.broadcasted_iota(jnp.int32, (TL, HID), 0)
    pieces = []
    for b in range(3):
        for a in range(3):
            taps = w2_raw[3 * a + b].astype(jnp.float32)
            pieces.append(
                jnp.where(
                    sub % 2 == 0,
                    jnp.broadcast_to(taps[0:1], (TL, HID)),
                    jnp.broadcast_to(taps[1:2], (TL, HID)),
                )
            )
    tall = jnp.concatenate(pieces, axis=0)
    wide = jnp.concatenate([tall, jnp.zeros((72, T * HID - HID), jnp.float32)], axis=1)
    state = (lax.broadcasted_iota(jnp.int32, (72, T * HID), 0) % TL) // 2
    total = jnp.where(state == 0, wide, 0.0)
    for t in range(1, T):
        total = total + jnp.where(state == t, pltpu.roll(wide, t * HID, 1), 0.0)
    w2[...] = total.astype(jnp.bfloat16)


def build_guide(count, obs_step, obs_row, obs_col, obs_value, guide):
    slot = lax.broadcasted_iota(jnp.int32, (1, SLOTS), 1)
    live = slot < count[0, 0]
    cell = jnp.where(live, obs_row[...] * TL + obs_step[...] * LAYERS, -1)
    hot = lax.broadcasted_iota(jnp.int32, (ROWS * TL, SLOTS), 0) == cell
    high, mid, low = three_parts(obs_value[...])
    left = jnp.concatenate(
        [
            jnp.where(hot, 1.0, 0.0),
            jnp.where(hot, high, 0.0),
            jnp.where(hot, mid, 0.0),
            jnp.where(hot, low, 0.0),
        ],
        axis=0,
    ).astype(jnp.bfloat16)
    right = jnp.where(
        lax.broadcasted_iota(jnp.int32, (COLS, SLOTS), 0) == obs_col[...], 1.0, 0.0
    ).astype(jnp.bfloat16)
    found = lax.dot_general(left, right, (((1,), (1,)), ((), ())), preferred_element_type=jnp.float32)
    rows = ROWS * TL
    guide[0:rows, :] = found[0:rows]
    guide[rows : 2 * rows, :] = (
        found[rows : 2 * rows] + found[2 * rows : 3 * rows] + found[3 * rows : 4 * rows]
    )


def kernel(
    sizes,
    x_hbm,
    first_hbm,
    second_hbm,
    w1_hbm,
    w2_hbm,
    embed_hbm,
    count,
    step_hbm,
    row_hbm,
    col_hbm,
    value_hbm,
    out,
    x_in,
    first,
    second,
    w1_raw,
    w2_raw,
    embed_raw,
    obs_step,
    obs_row,
    obs_col,
    obs_value,
    state,
    shift,
    slope,
    w1_turned,
    w1,
    w2,
    guide,
    tiles,
    frames,
    taps,
    load_sems,
    send_sems,
    recv_sems,
):
    n_tm, n_rows = sizes
    tm = lax.axis_index("tm")
    rw = lax.axis_index("rows")

    def peer(dt, dr):
        return {
            "tm": lax.rem(tm + dt + n_tm, n_tm) if dt else tm,
            "rows": lax.rem(rw + dr + n_rows, n_rows) if dr else rw,
        }

    barrier = pltpu.get_barrier_semaphore()
    for dt, dr in NEIGHBOURS:
        pl.semaphore_signal(barrier, inc=1, device_id=peer(dt, dr), device_id_type=MESH)

    loads = [
        pltpu.make_async_copy(src, dst, load_sems.at[i])
        for i, (src, dst) in enumerate(
            (
                (x_hbm, x_in),
                (w1_hbm, w1_raw),
                (embed_hbm, embed_raw),
                (w2_hbm, w2_raw),
                (step_hbm, obs_step),
                (row_hbm, obs_row),
                (col_hbm, obs_col),
                (value_hbm, obs_value),
                (first_hbm, first),
                (second_hbm, second),
            )
        )
    ]
    for load in loads:
        load.start()

    far_side = lax.rem(rw, 2)
    near_side = 1 - far_side

    def copy_to(index, k, dt, rows_to, source, target):
        return pltpu.make_async_remote_copy(
            src_ref=tiles.at[index, 1, source],
            dst_ref=tiles.at[index, 1 - dt, target],
            send_sem=send_sems.at[index, k],
            recv_sem=recv_sems.at[index, k],
            device_id={"tm": peer(dt, 0)["tm"], "rows": rows_to},
            device_id_type=MESH,
        )

    copies = []
    for index in range(2):
        made = []
        for side in (far_side, near_side):
            rows_to = lax.rem(rw + 2 * side - 1 + n_rows, n_rows)
            for dt in (-1, 1, 0):
                made.append(
                    copy_to(index, len(made), dt, rows_to, pl.ds(1 + side, 1), pl.ds(3 - 3 * side, 1))
                )
        for part in (slice(1, 3), slice(4, 6)):
            for dt in (-1, 1):
                made.append(copy_to(index, len(made), dt, rw, part, part))
        copies.append(made)

    def put_tiles(index, slot, upper, lower):
        scale = 1.0 / (1.0 + LEVELS[index] ** 2) ** 0.5
        tile = jnp.concatenate([upper, lower], axis=0) * scale
        tiles[index, 1, slot] = tile.astype(jnp.bfloat16)

    def unpack(index, slot, at_row, block):
        tile = tiles[index, block, slot].astype(jnp.float32)
        if block == 0:
            tile = jnp.where(tm == 0, 0.0, tile)
        if block == 2:
            tile = jnp.where(tm == n_tm - 1, 0.0, tile)
        for b in range(3):
            moved = pltpu.roll(tile, (1 - b) % COLS, 1) if b != 1 else tile
            for half in range(2):
                at = pl.multiple_of((at_row + half) * 72 + b * 24 + block * 8, 8)
                frames[pl.ds(at, 8), :] = moved[half * 8 : half * 8 + 8]

    def hidden_bands(index, group):
        ones = jnp.full((K_IN - 216, COLS), LEVELS[index], jnp.float32)
        windows = jnp.concatenate(
            [
                jnp.concatenate([frames[pl.ds(pl.multiple_of(72 * j, 8), 216), :], ones], axis=0).astype(
                    jnp.bfloat16
                )
                for j in group
            ],
            axis=1,
        )
        half = jnp.dot(w1[...], windows, preferred_element_type=jnp.float32)
        hidden = (half + half * jnp.tanh(half)).astype(jnp.bfloat16)
        found = jnp.dot(w2[...], hidden, preferred_element_type=jnp.float32)
        for k, j in enumerate(group):
            taps[j] = found[:, k * COLS : (k + 1) * COLS]

    def prepare_rows(index, noise):
        level_now, level_next = LEVELS[index], LEVELS[index + 1]
        base = 1.0 + level_now**2
        spread = level_now**2 - level_next**2
        keep = 1.0 / level_now**2
        gain = 1.0 / (OBS_NOISE + COVARIANCE_GAIN * level_now**2)
        turned = jnp.swapaxes(noise[...].reshape(TL, ROWS, COLS), 0, 1)
        for r in range(ROWS):
            current = state[r]
            hits = guide[r * 8 : r * 8 + 8, :]
            values = guide[64 + r * 8 : 64 + r * 8 + 8, :]
            still = current * (1.0 / base)
            score = (still - current) * keep + (values - hits * still) * gain
            shift[r] = current + spread * score + spread**0.5 * turned[r]
            slope[r] = (spread * level_now / base**0.5) * (keep - gain * hits)

    def finish_row(r):
        sums = [
            taps[r, b * 24 : b * 24 + 8, :]
            + taps[r + 1, b * 24 + 8 : b * 24 + 16, :]
            + taps[r + 2, b * 24 + 16 : b * 24 + 24, :]
            for b in range(3)
        ]
        net = sums[1] + pltpu.roll(sums[0], 1, 1) + pltpu.roll(sums[2], COLS - 1, 1)
        slab = shift[r] + slope[r] * net
        state[r] = slab
        return slab

    def finish_pair(index, pair, slot):
        slabs = [finish_row(2 * pair + half) for half in range(2)]
        if index == 0:
            put_tiles(1, slot, *slabs)

    def exchange_inner(index):
        for pair in range(1, 5):
            unpack(index, SLOT_OF[pair], 2 * pair, 1)
        for part in (EDGES, MIDS):
            for copy in copies[index][part]:
                copy.wait_recv()
        for pair in range(1, 5):
            unpack(index, SLOT_OF[pair], 2 * pair, 0)
            unpack(index, SLOT_OF[pair], 2 * pair, 2)
        hidden_bands(index, INNER_BANDS)
        for pair in (1, 2):
            finish_pair(index, pair, SLOT_OF[pair + 1])

    def exchange_outer(index, side, part):
        for copy in copies[index][part]:
            copy.wait_recv()
        for block in range(3):
            unpack(index, 3 * side, 10 * side, block)
        hidden_bands(index, (8 * side, 8 * side + 1))
        finish_pair(index, 3 * side, 1 + side)

    def start(index, part):
        for copy in copies[index][part]:
            copy.start()

    loads[0].wait()
    state[...] = jnp.swapaxes(x_in[...].reshape(TL, ROWS, COLS), 0, 1)
    for pair in range(4):
        put_tiles(0, SLOT_OF[pair + 1], state[2 * pair], state[2 * pair + 1])
    pl.semaphore_wait(barrier, len(NEIGHBOURS))
    start(0, FAR)
    for load in loads[1:]:
        load.wait()
    start(0, NEAR)
    build_conv_in(w1_raw, embed_raw, w1_turned, w1)
    start(0, EDGES)
    start(0, MIDS)
    build_conv_out(w2_raw, w2)
    build_guide(count, obs_step, obs_row, obs_col, obs_value, guide)
    prepare_rows(0, first)

    exchange_inner(0)
    start(1, MIDS)
    exchange_outer(0, near_side, NEAR)
    start(1, NEAR)
    exchange_outer(0, far_side, FAR)
    start(1, FAR)
    prepare_rows(1, second)
    start(1, EDGES)
    exchange_inner(1)
    exchange_outer(1, near_side, NEAR)
    for index in range(2):
        for copy in copies[index]:
            copy.wait_send()
    exchange_outer(1, far_side, FAR)
    out[...] = jnp.swapaxes(state[...], 0, 1).reshape(TL * ROWS, COLS)


def per_device(
    sizes,
    noisy_states,
    noise_first,
    noise_second,
    conv_in,
    conv_out,
    level_embed,
    obs_count,
    obs_step,
    obs_row,
    obs_col,
    obs_value,
):
    flat = (TL * ROWS, COLS)
    slots = (1, SLOTS)
    far = pl.BlockSpec(memory_space=pltpu.HBM)
    result = pl.pallas_call(
        functools.partial(kernel, sizes),
        out_shape=pltpu.VMEM(flat, jnp.float32),
        in_specs=[far] * 6 + [pl.BlockSpec(memory_space=pltpu.SMEM)] + [far] * 4,
        out_specs=pl.BlockSpec(memory_space=pltpu.VMEM),
        scratch_shapes=[
            pltpu.VMEM(flat, jnp.float32),
            pltpu.VMEM(flat, jnp.float32),
            pltpu.VMEM(flat, jnp.float32),
            pltpu.VMEM((9, C_IN, HID), jnp.bfloat16),
            pltpu.VMEM((9, LAYERS, HID), jnp.bfloat16),
            pltpu.VMEM((1, HID), jnp.float32),
            pltpu.VMEM(slots, jnp.int32),
            pltpu.VMEM(slots, jnp.int32),
            pltpu.VMEM(slots, jnp.int32),
            pltpu.VMEM(slots, jnp.float32),
            pltpu.VMEM((ROWS, TL, COLS), jnp.float32),
            pltpu.VMEM((ROWS, TL, COLS), jnp.float32),
            pltpu.VMEM((ROWS, TL, COLS), jnp.float32),
            pltpu.VMEM((256, 128), jnp.float32),
            pltpu.VMEM((T * HID, K_IN), jnp.bfloat16),
            pltpu.VMEM((72, T * HID), jnp.bfloat16),
            pltpu.VMEM((2 * ROWS * TL, COLS), jnp.float32),
            pltpu.VMEM((2, 3, PAIRS, 16, COLS), jnp.bfloat16),
            pltpu.VMEM((2 * PAIRS * 72, COLS), jnp.float32),
            pltpu.VMEM((BANDS, 72, COLS), jnp.float32),
            pltpu.SemaphoreType.DMA((10,)),
            pltpu.SemaphoreType.DMA((2, 10)),
            pltpu.SemaphoreType.DMA((2, 10)),
        ],
        compiler_params=pltpu.CompilerParams(
            collective_id=0, has_side_effects=True, vmem_limit_bytes=32 * 1024 * 1024
        ),
        name="reverse_steps",
    )(
        *(
            operand if operand is obs_count else pltpu.with_memory_space_constraint(operand, pltpu.HBM)
            for operand in (
                noisy_states.reshape(flat),
                noise_first.reshape(flat),
                noise_second.reshape(flat),
                jnp.swapaxes(conv_in, 1, 2),
                conv_out,
                level_embed.reshape(1, HID),
                obs_count,
                obs_step.reshape(slots),
                obs_row.reshape(slots),
                obs_col.reshape(slots),
                obs_value.reshape(slots),
            )
        )
    )
    return result.reshape(noisy_states.shape)


def solution(mesh):
    sizes = (mesh.shape["tm"], mesh.shape["rows"])
    cells = P("tm", None, "rows", None)
    block = P("tm", "rows", None)
    return jax.shard_map(
        functools.partial(per_device, sizes),
        mesh=mesh,
        in_specs=(cells, cells, cells, P(), P(), P(), P("tm", "rows"), block, block, block, block),
        out_specs=cells,
        check_vma=False,
    )
```

```python
import functools

import jax
import jax.numpy as jnp
from jax import lax
from jax.experimental import pallas as pl
from jax.experimental.pallas import tpu as pltpu
from jax.sharding import PartitionSpec as P

MESH = pl.DeviceIdType.MESH
LEVELS = (1.0, 0.5, 0.2)
OBS_NOISE = 0.1
COVARIANCE_GAIN = 0.5
T = 4
LAYERS = 2
TL = 8
ROWS = 8
COLS = 256
HID = 96
C_IN = 18
SLOTS = 256
PAIRS = 6
BANDS = 10
K_IN = 224
NEIGHBOURS = ((0, -1), (0, 1), (-1, -1), (1, -1), (-1, 1), (1, 1), (-1, 0), (1, 0))
SLOT_OF = (0, 1, 4, 5, 2, 3)
FAR, NEAR, EDGES, MIDS = slice(0, 3), slice(3, 6), slice(6, 8), slice(8, 10)
INNER_BANDS = (4, 5, 2, 3, 6, 7)


def three_parts(values):
    high = values.astype(jnp.bfloat16).astype(jnp.float32)
    rest = values - high
    mid = rest.astype(jnp.bfloat16).astype(jnp.float32)
    return high, mid, rest - mid


def build_conv_in(w1_raw, embed_raw, w1_turned, w1):
    w1_turned[...] = jnp.zeros(w1_turned.shape, jnp.float32)
    for off in range(9):
        w1_turned[24 * off : 24 * off + C_IN, 0:HID] = w1_raw[off].astype(jnp.float32) * 0.5
    parts = three_parts(embed_raw[...] * 0.5)
    for piece in range(3):
        w1_turned[216 + piece : 217 + piece, 0:HID] = parts[piece]
    base = jnp.transpose(w1_turned[...])[:HID]
    lane = lax.broadcasted_iota(jnp.int32, (HID, 256), 1)
    for t in range(T):
        shifted = jnp.where(lane < 216, pltpu.roll(base, 2 * t, 1), base) if t else base
        w1[t * HID : (t + 1) * HID, :] = shifted[:, :K_IN].astype(jnp.bfloat16)


def build_conv_out(w2_raw, w2):
    sub = lax.broadcasted_iota(jnp.int32, (TL, HID), 0)
    pieces = []
    for b in range(3):
        for a in range(3):
            taps = w2_raw[3 * a + b].astype(jnp.float32)
            pieces.append(
                jnp.where(
                    sub % 2 == 0,
                    jnp.broadcast_to(taps[0:1], (TL, HID)),
                    jnp.broadcast_to(taps[1:2], (TL, HID)),
                )
            )
    tall = jnp.concatenate(pieces, axis=0)
    wide = jnp.concatenate([tall, jnp.zeros((72, T * HID - HID), jnp.float32)], axis=1)
    state = (lax.broadcasted_iota(jnp.int32, (72, T * HID), 0) % TL) // 2
    total = jnp.where(state == 0, wide, 0.0)
    for t in range(1, T):
        total = total + jnp.where(state == t, pltpu.roll(wide, t * HID, 1), 0.0)
    w2[...] = total.astype(jnp.bfloat16)


def build_guide(count, obs_step, obs_row, obs_col, obs_value, guide):
    slot = lax.broadcasted_iota(jnp.int32, (1, SLOTS), 1)
    live = slot < count[0, 0]
    cell = jnp.where(live, obs_row[...] * TL + obs_step[...] * LAYERS, -1)
    hot = lax.broadcasted_iota(jnp.int32, (ROWS * TL, SLOTS), 0) == cell
    high, mid, low = three_parts(obs_value[...])
    left = jnp.concatenate(
        [
            jnp.where(hot, 1.0, 0.0),
            jnp.where(hot, high, 0.0),
            jnp.where(hot, mid, 0.0),
            jnp.where(hot, low, 0.0),
        ],
        axis=0,
    ).astype(jnp.bfloat16)
    right = jnp.where(
        lax.broadcasted_iota(jnp.int32, (COLS, SLOTS), 0) == obs_col[...], 1.0, 0.0
    ).astype(jnp.bfloat16)
    found = lax.dot_general(left, right, (((1,), (1,)), ((), ())), preferred_element_type=jnp.float32)
    rows = ROWS * TL
    guide[0:rows, :] = found[0:rows]
    guide[rows : 2 * rows, :] = (
        found[rows : 2 * rows] + found[2 * rows : 3 * rows] + found[3 * rows : 4 * rows]
    )


def kernel(
    sizes,
    x_hbm,
    first_hbm,
    second_hbm,
    w1_hbm,
    w2_hbm,
    embed_hbm,
    count,
    step_hbm,
    row_hbm,
    col_hbm,
    value_hbm,
    out,
    x_in,
    first,
    second,
    w1_raw,
    w2_raw,
    embed_raw,
    obs_step,
    obs_row,
    obs_col,
    obs_value,
    state,
    shift,
    slope,
    w1_turned,
    w1,
    w2,
    guide,
    tiles,
    frames,
    taps,
    load_sems,
    send_sems,
    recv_sems,
):
    n_tm, n_rows = sizes
    tm = lax.axis_index("tm")
    rw = lax.axis_index("rows")

    def peer(dt, dr):
        return {
            "tm": lax.rem(tm + dt + n_tm, n_tm) if dt else tm,
            "rows": lax.rem(rw + dr + n_rows, n_rows) if dr else rw,
        }

    barrier = pltpu.get_barrier_semaphore()
    far_to = lax.rem(rw + 2 * lax.rem(rw, 2) - 1 + n_rows, n_rows)
    near_to = lax.rem(rw + 1 - 2 * lax.rem(rw, 2) + n_rows, n_rows)
    for rows_to in (far_to, near_to, rw):
        for dt in (0, -1, 1):
            if dt or rows_to is not rw:
                pl.semaphore_signal(
                    barrier,
                    inc=1,
                    device_id={"tm": peer(dt, 0)["tm"], "rows": rows_to},
                    device_id_type=MESH,
                )

    loads = [
        pltpu.make_async_copy(src, dst, load_sems.at[i])
        for i, (src, dst) in enumerate(
            (
                (x_hbm, x_in),
                (w1_hbm, w1_raw),
                (embed_hbm, embed_raw),
                (w2_hbm, w2_raw),
                (step_hbm, obs_step),
                (row_hbm, obs_row),
                (col_hbm, obs_col),
                (value_hbm, obs_value),
                (first_hbm, first),
                (second_hbm, second),
            )
        )
    ]
    for load in loads:
        load.start()

    far_side = lax.rem(rw, 2)
    near_side = 1 - far_side

    def copy_to(index, k, dt, rows_to, source, target):
        return pltpu.make_async_remote_copy(
            src_ref=tiles.at[index, 1, source],
            dst_ref=tiles.at[index, 1 - dt, target],
            send_sem=send_sems.at[index, k],
            recv_sem=recv_sems.at[index, k],
            device_id={"tm": peer(dt, 0)["tm"], "rows": rows_to},
            device_id_type=MESH,
        )

    copies = []
    for index in range(2):
        made = []
        for side in (far_side, near_side):
            rows_to = lax.rem(rw + 2 * side - 1 + n_rows, n_rows)
            for dt in (-1, 1, 0):
                made.append(
                    copy_to(index, len(made), dt, rows_to, pl.ds(1 + side, 1), pl.ds(3 - 3 * side, 1))
                )
        for part in (slice(1, 3), slice(4, 6)):
            for dt in (-1, 1):
                made.append(copy_to(index, len(made), dt, rw, part, part))
        copies.append(made)

    def put_tiles(index, slot, upper, lower):
        scale = 1.0 / (1.0 + LEVELS[index] ** 2) ** 0.5
        tile = jnp.concatenate([upper, lower], axis=0) * scale
        tiles[index, 1, slot] = tile.astype(jnp.bfloat16)

    def unpack(index, slot, at_row, block):
        tile = tiles[index, block, slot].astype(jnp.float32)
        if block == 0:
            tile = jnp.where(tm == 0, 0.0, tile)
        if block == 2:
            tile = jnp.where(tm == n_tm - 1, 0.0, tile)
        for b in range(3):
            moved = pltpu.roll(tile, (1 - b) % COLS, 1) if b != 1 else tile
            for half in range(2):
                at = pl.multiple_of((at_row + half) * 72 + b * 24 + block * 8, 8)
                frames[pl.ds(at, 8), :] = moved[half * 8 : half * 8 + 8]

    def hidden_bands(index, group):
        ones = jnp.full((K_IN - 216, COLS), LEVELS[index], jnp.float32)
        windows = jnp.concatenate(
            [
                jnp.concatenate([frames[pl.ds(pl.multiple_of(72 * j, 8), 216), :], ones], axis=0).astype(
                    jnp.bfloat16
                )
                for j in group
            ],
            axis=1,
        )
        half = jnp.dot(w1[...], windows, preferred_element_type=jnp.float32)
        hidden = (half + half * jnp.tanh(half)).astype(jnp.bfloat16)
        found = jnp.dot(w2[...], hidden, preferred_element_type=jnp.float32)
        for k, j in enumerate(group):
            taps[j] = found[:, k * COLS : (k + 1) * COLS]

    def prepare_rows(index, noise):
        level_now, level_next = LEVELS[index], LEVELS[index + 1]
        base = 1.0 + level_now**2
        spread = level_now**2 - level_next**2
        keep = 1.0 / level_now**2
        gain = 1.0 / (OBS_NOISE + COVARIANCE_GAIN * level_now**2)
        turned = jnp.swapaxes(noise[...].reshape(TL, ROWS, COLS), 0, 1)
        for r in range(ROWS):
            current = state[r]
            hits = guide[r * 8 : r * 8 + 8, :]
            values = guide[64 + r * 8 : 64 + r * 8 + 8, :]
            still = current * (1.0 / base)
            score = (still - current) * keep + (values - hits * still) * gain
            shift[r] = current + spread * score + spread**0.5 * turned[r]
            slope[r] = (spread * level_now / base**0.5) * (keep - gain * hits)

    def finish_row(r):
        sums = [
            taps[r, b * 24 : b * 24 + 8, :]
            + taps[r + 1, b * 24 + 8 : b * 24 + 16, :]
            + taps[r + 2, b * 24 + 16 : b * 24 + 24, :]
            for b in range(3)
        ]
        net = sums[1] + pltpu.roll(sums[0], 1, 1) + pltpu.roll(sums[2], COLS - 1, 1)
        slab = shift[r] + slope[r] * net
        state[r] = slab
        return slab

    def finish_pair(index, pair, slot):
        slabs = [finish_row(2 * pair + half) for half in range(2)]
        if index == 0:
            put_tiles(1, slot, *slabs)

    def exchange_inner(index):
        for pair in range(1, 5):
            unpack(index, SLOT_OF[pair], 2 * pair, 1)
        for part in (EDGES, MIDS):
            for copy in copies[index][part]:
                copy.wait_recv()
        for pair in range(1, 5):
            unpack(index, SLOT_OF[pair], 2 * pair, 0)
            unpack(index, SLOT_OF[pair], 2 * pair, 2)
        hidden_bands(index, INNER_BANDS)
        for pair in (1, 2):
            finish_pair(index, pair, SLOT_OF[pair + 1])

    def exchange_outer(index, side, part):
        for copy in copies[index][part]:
            copy.wait_recv()
        for block in range(3):
            unpack(index, 3 * side, 10 * side, block)
        hidden_bands(index, (8 * side, 8 * side + 1))
        finish_pair(index, 3 * side, 1 + side)

    def start(index, part):
        for copy in copies[index][part]:
            copy.start()

    loads[0].wait()
    state[...] = jnp.swapaxes(x_in[...].reshape(TL, ROWS, COLS), 0, 1)
    for pair in range(4):
        put_tiles(0, SLOT_OF[pair + 1], state[2 * pair], state[2 * pair + 1])
    pl.semaphore_wait(barrier, len(NEIGHBOURS))
    start(0, FAR)
    for load in loads[1:]:
        load.wait()
    start(0, NEAR)
    build_conv_in(w1_raw, embed_raw, w1_turned, w1)
    start(0, EDGES)
    start(0, MIDS)
    build_conv_out(w2_raw, w2)
    build_guide(count, obs_step, obs_row, obs_col, obs_value, guide)
    prepare_rows(0, first)

    exchange_inner(0)
    start(1, MIDS)
    exchange_outer(0, near_side, NEAR)
    start(1, NEAR)
    exchange_outer(0, far_side, FAR)
    start(1, FAR)
    start(1, EDGES)
    prepare_rows(1, second)
    exchange_inner(1)
    exchange_outer(1, near_side, NEAR)
    for index in range(2):
        for copy in copies[index]:
            copy.wait_send()
    exchange_outer(1, far_side, FAR)
    out[...] = jnp.swapaxes(state[...], 0, 1).reshape(TL * ROWS, COLS)


def per_device(
    sizes,
    noisy_states,
    noise_first,
    noise_second,
    conv_in,
    conv_out,
    level_embed,
    obs_count,
    obs_step,
    obs_row,
    obs_col,
    obs_value,
):
    flat = (TL * ROWS, COLS)
    slots = (1, SLOTS)
    far = pl.BlockSpec(memory_space=pltpu.HBM)
    result = pl.pallas_call(
        functools.partial(kernel, sizes),
        out_shape=pltpu.VMEM(flat, jnp.float32),
        in_specs=[far] * 6 + [pl.BlockSpec(memory_space=pltpu.SMEM)] + [far] * 4,
        out_specs=pl.BlockSpec(memory_space=pltpu.VMEM),
        scratch_shapes=[
            pltpu.VMEM(flat, jnp.float32),
            pltpu.VMEM(flat, jnp.float32),
            pltpu.VMEM(flat, jnp.float32),
            pltpu.VMEM((9, C_IN, HID), jnp.bfloat16),
            pltpu.VMEM((9, LAYERS, HID), jnp.bfloat16),
            pltpu.VMEM((1, HID), jnp.float32),
            pltpu.VMEM(slots, jnp.int32),
            pltpu.VMEM(slots, jnp.int32),
            pltpu.VMEM(slots, jnp.int32),
            pltpu.VMEM(slots, jnp.float32),
            pltpu.VMEM((ROWS, TL, COLS), jnp.float32),
            pltpu.VMEM((ROWS, TL, COLS), jnp.float32),
            pltpu.VMEM((ROWS, TL, COLS), jnp.float32),
            pltpu.VMEM((256, 128), jnp.float32),
            pltpu.VMEM((T * HID, K_IN), jnp.bfloat16),
            pltpu.VMEM((72, T * HID), jnp.bfloat16),
            pltpu.VMEM((2 * ROWS * TL, COLS), jnp.float32),
            pltpu.VMEM((2, 3, PAIRS, 16, COLS), jnp.bfloat16),
            pltpu.VMEM((2 * PAIRS * 72, COLS), jnp.float32),
            pltpu.VMEM((BANDS, 72, COLS), jnp.float32),
            pltpu.SemaphoreType.DMA((10,)),
            pltpu.SemaphoreType.DMA((2, 10)),
            pltpu.SemaphoreType.DMA((2, 10)),
        ],
        compiler_params=pltpu.CompilerParams(
            collective_id=0, has_side_effects=True, vmem_limit_bytes=32 * 1024 * 1024
        ),
        name="reverse_steps",
    )(
        *(
            operand if operand is obs_count else pltpu.with_memory_space_constraint(operand, pltpu.HBM)
            for operand in (
                noisy_states.reshape(flat),
                noise_first.reshape(flat),
                noise_second.reshape(flat),
                jnp.swapaxes(conv_in, 1, 2),
                conv_out,
                level_embed.reshape(1, HID),
                obs_count,
                obs_step.reshape(slots),
                obs_row.reshape(slots),
                obs_col.reshape(slots),
                obs_value.reshape(slots),
            )
        )
    )
    return result.reshape(noisy_states.shape)


def solution(mesh):
    sizes = (mesh.shape["tm"], mesh.shape["rows"])
    cells = P("tm", None, "rows", None)
    block = P("tm", "rows", None)
    return jax.shard_map(
        functools.partial(per_device, sizes),
        mesh=mesh,
        in_specs=(cells, cells, cells, P(), P(), P(), P("tm", "rows"), block, block, block, block),
        out_specs=cells,
        check_vma=False,
    )
```
